256 devices in a mesh: pair: 8 (over x, core), virt: 32 (over y, z).
Axes of the slice: x: 4, y: 4, z: 8, core: 2. Of those that a mesh axis runs over, the one named last changes fastest.
Arguments:
- amplitudes: bfloat16 [640, 320, 320], P('pair', 'virt'), may hold values from -6 to 6
- integrals: bfloat16 [320, 320, 16, 320], P('virt', 'pair'), may hold values from -0.109375 to 0.109375
- virt_irrep: int32 [320], replicated, may hold values from 0 to 7
- tile_irrep: int32 [16], replicated, may hold values from 0 to 7
- pair_irrep: int32 [640], replicated, may hold values from 0 to 7
Outputs:
- ladder: float32 [640, 16, 320], P('pair', None, 'virt')
The draws below stay inside these ranges and needn't reach their ends.
All inputs are finite; a program needn't handle non-finite values.
Results may differ from the reference program's by a relative error of at most 0.0003.
Values may be sent and summed in bfloat16 or wider, within the bound.
No kernel may reach another device: no remote copies, remote signals or barrier semaphores. Data moves between devices by JAX's collectives and lax.ppermute only.
A program may use at most 128 MiB of HBM per device.

```python
import math
import jax
import jax.numpy as jnp
import numpy as np
from jax import lax

NV = 320
NB = 16
PAIRS = 640


def place_ends(drawn, rng, smallest, largest):
    index_at = [jax.random.randint(jax.random.fold_in(rng, axis), (), 0, length) for axis, length in enumerate(drawn.shape)]
    main_axis = drawn.shape.index(max(drawn.shape))
    neighbour = index_at[:main_axis] + [(index_at[main_axis] + 1) % drawn.shape[main_axis]] + index_at[main_axis + 1:]
    return drawn.at[tuple(index_at)].set(smallest).at[tuple(neighbour)].set(largest)


def raised(array, own_key, source, target, shards_of, factor):
    def block_of(dim):
        return (jnp.arange(array.shape[dim]) // (array.shape[dim] // shards_of)).reshape((-1,) + (1,) * (array.ndim - 1 - dim))

    near = jax.random.permutation(own_key, shards_of)[block_of(target)]
    other_side = (block_of(target) + shards_of // 2) % shards_of
    return jnp.where((block_of(source) == near) | (block_of(source) == other_side), factor * array, array)


def steps_of(key, extent, shards, low, high):
    def one(axis_at, parts):
        steps = jax.random.uniform(jax.random.fold_in(jax.random.fold_in(key, 6), axis_at), (parts,), jnp.float32, low / len(shards), high / len(shards))
        return jnp.repeat(jnp.exp(steps), extent[axis_at] // parts).reshape((-1,) + (1,) * (len(extent) - axis_at - 1))

    factor_of = one(*shards[0])
    for cut in shards[1:]:
        factor_of = factor_of * one(*cut)
    return factor_of


def rank_bounds(number_of, lean):
    loads = [(1 << 20) // math.isqrt(rank ** lean) + 1 for rank in range(1, number_of + 1)]
    width = 1 + sum(loads) // (1 << 30)
    return np.cumsum(np.array([max(1, weight // width) for weight in loads]))


def ranked(stream_key, extent, count, lean):
    table = rank_bounds(count, lean)
    ticket = jax.random.randint(jax.random.fold_in(stream_key, 1), extent, 0, int(table[count - 1]))
    grade = jnp.searchsorted(jnp.asarray(table, jnp.int32), ticket, side="right")
    return jax.random.permutation(jax.random.fold_in(stream_key, 2), count)[grade].astype(jnp.int32)


def normal_values(own_key, shape, deviation, bound, cuts=(), held_as=jnp.bfloat16):
    drawn = deviation * jax.random.normal(own_key, shape, jnp.float32)
    if cuts:
        drawn = drawn * steps_of(own_key, shape, cuts, -0.22, 0.18)
    return jnp.clip(drawn, -bound, bound).astype(held_as)


def gaussian_with(key, extent, scale, limit, shards, heavy, held_as=jnp.bfloat16):
    result = scale * jax.random.normal(key, extent, jnp.float32)
    if shards:
        result = result * steps_of(key, extent, shards, -0.22, 0.18)
    return jnp.clip(raised(result, jax.random.fold_in(key, 3), *heavy), -limit, limit).astype(held_as)


def setup_inputs(seed: int = 0) -> dict:
    splits = jax.random.split(jax.random.key(seed), 6)
    amplitudes = normal_values(splits[0], (PAIRS, NV, NV), 1.0, 6.0, ((0, 8), (1, 32)))
    integrals = gaussian_with(splits[1], (NV, NV, NB, NV), (NV * NV // 8) ** -0.5, 0.109375, ((0, 32), (1, 8)), (0, 3, 32, 2.75))
    virt_irrep = place_ends(ranked(splits[2], (NV,), 8, 2), jax.random.fold_in(splits[2], 3), 0, 7).astype(jnp.int32)
    tile_irrep = place_ends(ranked(splits[3], (NB,), 8, 2), jax.random.fold_in(splits[3], 3), 0, 7).astype(jnp.int32)
    pair_irrep = place_ends(jax.random.randint(splits[4], (PAIRS,), 0, 8), jax.random.fold_in(splits[4], 1), 0, 7).astype(jnp.int32)
    return {"amplitudes": amplitudes, "integrals": integrals, "virt_irrep": virt_irrep, "tile_irrep": tile_irrep, "pair_irrep": pair_irrep}


def reference(amplitudes, integrals, virt_irrep, tile_irrep, pair_irrep):
    pair_sym = jnp.bitwise_xor(virt_irrep[:, None], virt_irrep[None, :])
    amp_keep = pair_sym[None] == pair_irrep[:, None, None]
    masked_amp = jnp.where(amp_keep, amplitudes, jnp.zeros_like(amplitudes))
    tile_sym = jnp.bitwise_xor(tile_irrep[:, None], virt_irrep[None, :])
    amp_rows = jnp.swapaxes(masked_amp, 0, 1)

    def one_orbital(running, pieces):
        int_slab, amp_slab, row_sym = pieces
        int_keep = row_sym[:, None, None] == tile_sym[None]
        masked = jnp.where(int_keep, int_slab, jnp.zeros_like(int_slab))
        added = jnp.dot(amp_slab, masked.reshape(NV, NB * NV), preferred_element_type=jnp.float32)
        return running + added, None

    start_sum = jnp.zeros((PAIRS, NB * NV), jnp.float32)
    summed = lax.scan(one_orbital, start_sum, (integrals, amp_rows, pair_sym))[0]
    return summed.reshape(PAIRS, NB, NV)
```

```python
import functools

import jax
import jax.numpy as jnp
from jax import lax
from jax.experimental import pallas as pl
from jax.experimental.pallas import tpu as pltpu
from jax.sharding import PartitionSpec as P

F32 = jnp.float32
BF16 = jnp.bfloat16
I32 = jnp.int32
SLOTS = 24
CHIPS = 4
CORES = 2
OWNERS = CHIPS * CORES
COLUMNS = 32
ROWS = 80
OWN_C = 10
OWN_D = 40
OWN_A = 10
TILE = 16
HALF = TILE // 2
WIDTH = 320
DEPTH = OWN_C * OWN_D
DEPTH_PAD = 512
WORDS = HALF * WIDTH
MESSAGE = WORDS + 128
CORE_ROWS = CHIPS * SLOTS
FINE = 64.0
FULL = 32767.0
VMEM = pl.BlockSpec(memory_space=pltpu.VMEM)
SMEM = pl.BlockSpec(memory_space=pltpu.SMEM)


def params():
    return pltpu.CompilerParams(vmem_limit_bytes=40 * 1024 * 1024)


def iota(shape, axis):
    return lax.broadcasted_iota(I32, shape, axis)


def local_labels(pairs_ref):
    owner = lax.axis_index("pair")
    row = pairs_ref[:, 0:ROWS]
    for k in range(1, OWNERS):
        row = jnp.where(owner == k, pairs_ref[:, k * ROWS : (k + 1) * ROWS], row)
    return row


def slots_of(row, round_index):
    first, second = iota((ROWS, ROWS), 0), iota((ROWS, ROWS), 1)
    spread = jnp.broadcast_to(row.astype(F32), (ROWS, ROWS))
    column = jnp.sum(jnp.where(first == second, spread, 0.0), axis=1, keepdims=True)
    before = (column == spread) & (first < second)
    rank = jnp.sum(jnp.where(before, 1.0, 0.0), axis=0, keepdims=True)
    slot = rank - (round_index * SLOTS).astype(F32)
    hot = iota((SLOTS, ROWS), 0).astype(F32) == slot
    return column, jnp.where(hot, 1.0, 0.0)


def pack_kernel(round_ref, virt_s, virt_v, pairs_v, amp_ref, out_ref, wide):
    row = local_labels(pairs_v)
    column, hot = slots_of(row, round_ref[0])
    hot = hot.astype(BF16)
    column = column.astype(I32)
    base = lax.axis_index("virt") * OWN_C
    wide[:, :, 384:DEPTH_PAD] = jnp.zeros((OWNERS, SLOTS, DEPTH_PAD - 384), F32)
    for c in range(OWN_C):
        key = jnp.bitwise_xor(virt_v[...], virt_s[base + c])
        kept = jnp.where(column == key, amp_ref[c].astype(F32), 0.0).astype(BF16)
        packed = jnp.dot(hot, kept, preferred_element_type=F32)
        for owner in range(OWNERS):
            wide[owner, :, c * OWN_D : (c + 1) * OWN_D] = packed[:, owner * OWN_D : (owner + 1) * OWN_D]
    out_ref[...] = wide[...].astype(BF16)


def tile_column(tile_s):
    column = jnp.zeros((TILE, 1), I32)
    place = iota((TILE, 1), 0)
    for b in range(TILE):
        column = jnp.where(place == b, tile_s[b], column)
    return column


def mask_kernel(virt_s, tile_s, virt_v, int_ref, out_ref, masks, turn):
    step = pl.program_id(0)

    @pl.when(step == 0)
    def _():
        label = jnp.bitwise_xor(tile_column(tile_s), virt_v[...])
        for g in range(8):
            masks[g] = jnp.where(label == g, 1.0, 0.0).astype(BF16)
        high, low = iota((256, 256), 0), iota((256, 256), 1)
        match = (high // 16 == low % 16) & (high % 16 == low // 16)
        turn[...] = jnp.where(match, 1.0, 0.0).astype(BF16)

    base_c = lax.axis_index("virt") * OWN_C + step * 2
    base_d = lax.axis_index("pair") * OWN_D
    for group in range(5):
        slabs = []
        for k in range(16):
            c, d = divmod(group * 16 + k, OWN_D)
            g = jnp.bitwise_xor(virt_s[base_c + c], virt_s[base_d + d])
            slabs.append(int_ref[c, d] * masks[g])
        turned = jnp.dot(turn[...], jnp.concatenate(slabs, axis=0), preferred_element_type=F32).astype(BF16)
        for b in range(TILE):
            out_ref[b, group * 16 : (group + 1) * 16, :] = turned[b * 16 : (b + 1) * 16]


def left_rows(amp_ref, core, left):
    for x in range(CHIPS):
        left[x * SLOTS : (x + 1) * SLOTS, :] = amp_ref[2 * x + core].astype(F32)
    return left[...].astype(BF16)[:, :DEPTH]


def scale_code(largest):
    return jnp.ceil(FINE * jnp.log2(jnp.maximum(largest, 1e-36))).astype(I32)


def scale_up(code):
    return FULL * jnp.exp2(code.astype(F32) * (-1.0 / FINE))


def scale_down(code):
    return jnp.exp2(code.astype(F32) * (1.0 / FINE)) * (1.0 / FULL)


def joined(high, low, factor):
    high = jnp.round(high * factor).astype(I32)
    low = jnp.round(low * factor).astype(I32)
    return jnp.left_shift(high, 16) | (low & 0xFFFF)


def high_of(word):
    return jnp.right_shift(word, 16).astype(F32)


def low_of(word):
    return jnp.right_shift(jnp.left_shift(word, 16), 16).astype(F32)


def row_largest(values):
    top = jnp.abs(values[0])
    for b in range(1, TILE):
        top = jnp.maximum(top, jnp.abs(values[b]))
    return jnp.max(top, axis=1, keepdims=True)


def write_words(values, out_ref):
    code = scale_code(row_largest(values))
    factor = scale_up(code)
    for b in range(HALF):
        out_ref[:, b * WIDTH : (b + 1) * WIDTH] = joined(values[b], values[b + HALF], factor)
    out_ref[:, WORDS:MESSAGE] = jnp.broadcast_to(code, (code.shape[0], MESSAGE - WORDS))


def send_kernel(amp_ref, int_ref, out_ref, left, values):
    other = 1 - lax.axis_index("pair") % CORES
    rows = left_rows(amp_ref, other, left)
    for b in range(TILE):
        values[b] = jnp.dot(rows, int_ref[b], preferred_element_type=F32)
    write_words(values, out_ref)


def keep_kernel(amp_ref, int_ref, out_ref, left):
    rows = left_rows(amp_ref, lax.axis_index("pair") % CORES, left)
    for b in range(TILE):
        out_ref[b] = jnp.dot(rows, int_ref[b], preferred_element_type=F32)


def add_words(words, values, start):
    factor = scale_down(words[:, WORDS : WORDS + 1])
    for b in range(HALF):
        word = words[:, b * WIDTH : (b + 1) * WIDTH]
        values[b] = start[b] + high_of(word) * factor
        values[b + HALF] = start[b + HALF] + low_of(word) * factor


def chip_kernel(keep_ref, got_ref, own_ref, one_ref, two_ref, three_ref, values, words):
    add_words(got_ref, values, keep_ref)
    write_words(values, words)
    x = lax.axis_index("pair") // CORES
    for hop, out in ((1, one_ref), (2, two_ref), (3, three_ref)):
        start = pl.multiple_of(lax.rem(x + hop, CHIPS) * SLOTS, 8)
        out[...] = words[pl.ds(start, SLOTS), :]
    start = pl.multiple_of(x * SLOTS, 8)
    for b in range(TILE):
        own_ref[b] = values[b, pl.ds(start, SLOTS), :]


def piece(group, b):
    index = group * HALF + b
    return 8 * (index // 12), OWN_A * (index % 12)


def column_kernel(own_ref, one_ref, two_ref, three_ref, out_ref, values, words):
    add_words(one_ref, values, own_ref)
    add_words(two_ref, values, values)
    add_words(three_ref, values, values)
    write_words(values, words)
    code = words[:, WORDS : WORDS + 8]
    lane = iota((8, 8), 1)
    tail = jnp.where(lane == 0, code[0:8], jnp.where(lane == 1, code[8:16], code[16:24]))
    for j in range(COLUMNS):
        for group in range(SLOTS // 8):
            for b in range(HALF):
                row, lane_at = piece(group, b)
                start = b * WIDTH + j * OWN_A
                out_ref[j, row : row + 8, lane_at : lane_at + OWN_A] = words[
                    group * 8 : group * 8 + 8, start : start + OWN_A
                ]
        out_ref[j, 0:8, 120:128] = tail
        out_ref[j, 8:16, 120:128] = tail


def final_kernel(round_ref, virt_s, tile_s, pairs_v, got_ref, out_ref, flat):
    row = local_labels(pairs_v)
    _, hot = slots_of(row, round_ref[0])
    lane = iota((8, 128), 1)
    sums = [[jnp.zeros((8, 128), F32) for _ in range(2)] for _ in range(2)]
    for j in range(COLUMNS):
        for block in range(2):
            word = got_ref[j, 8 * block : 8 * block + 8, :]
            if block == 0:
                code = jnp.where(lane < 80, word[:, 120:121], word[:, 121:122])
            else:
                code = jnp.where(lane < 40, word[:, 121:122], word[:, 122:123])
            factor = scale_down(code)
            sums[0][block] += high_of(word) * factor
            sums[1][block] += low_of(word) * factor
    for half in range(2):
        for group in range(SLOTS // 8):
            for b in range(HALF):
                at, lane_at = piece(group, b)
                to = (half * HALF + b) * OWN_A
                flat[group * 8 : group * 8 + 8, to : to + OWN_A] = sums[half][at // 8][:, lane_at : lane_at + OWN_A]
    spread = lax.dot_general(
        flat[...], hot, (((0,), (0,)), ((), ())), precision=lax.Precision.HIGHEST, preferred_element_type=F32
    )
    base = lax.axis_index("virt") * OWN_A
    column = tile_column(tile_s)
    for a in range(OWN_A):
        for b in range(TILE):
            out_ref[a, b : b + 1, :] = spread[b * OWN_A + a : b * OWN_A + a + 1]
        keep = jnp.bitwise_xor(column, virt_s[base + a]) == row
        out_ref[a] = jnp.where(keep, out_ref[a], 0.0)


def shape(dims, dtype):
    return jax.ShapeDtypeStruct(dims, dtype)


def masked_integrals(integrals, virt, tile, virt_row):
    return pl.pallas_call(
        mask_kernel,
        out_shape=shape((TILE, DEPTH, WIDTH), BF16),
        grid=(OWN_C // 2,),
        in_specs=[
            SMEM,
            SMEM,
            pl.BlockSpec((1, WIDTH), lambda s: (0, 0)),
            pl.BlockSpec((2, OWN_D, TILE, WIDTH), lambda s: (s, 0, 0, 0)),
        ],
        out_specs=pl.BlockSpec((TILE, 2 * OWN_D, WIDTH), lambda s: (0, s, 0)),
        scratch_shapes=[pltpu.VMEM((8, TILE, WIDTH), BF16), pltpu.VMEM((256, 256), BF16)],
        compiler_params=params(),
        name="mask_turn",
        cost_estimate=pl.CostEstimate(flops=1 << 30, bytes_accessed=10 << 20, transcendentals=0),
    )(virt, tile, virt_row, integrals)


def one_round(round_index, amplitudes, integrals, virt, tile, pairs):
    virt_row = virt.reshape(1, WIDTH)
    pair_row = pairs.reshape(1, OWNERS * ROWS)
    number = jnp.reshape(round_index, (1,)).astype(I32)
    packed = pl.pallas_call(
        pack_kernel,
        out_shape=shape((OWNERS, SLOTS, DEPTH_PAD), BF16),
        in_specs=[SMEM, SMEM, VMEM, VMEM, VMEM],
        out_specs=VMEM,
        scratch_shapes=[pltpu.VMEM((OWNERS, SLOTS, DEPTH_PAD), F32)],
        compiler_params=params(),
        name="pack",
    )(number, virt, virt_row, pair_row, jnp.transpose(amplitudes, (1, 0, 2)))
    amp = lax.all_to_all(packed, "pair", split_axis=0, concat_axis=0, tiled=True)
    ints = masked_integrals(integrals, virt, tile, virt_row)
    left = pltpu.VMEM((CORE_ROWS, DEPTH_PAD), F32)
    table = pltpu.VMEM((TILE, CORE_ROWS, WIDTH), F32)
    send = pl.pallas_call(
        send_kernel,
        out_shape=shape((CORE_ROWS, MESSAGE), I32),
        in_specs=[VMEM, VMEM],
        out_specs=VMEM,
        scratch_shapes=[left, table],
        compiler_params=params(),
        name="send_rows",
    )(amp, ints)
    got = lax.ppermute(send, "pair", [(i, i ^ 1) for i in range(OWNERS)])
    keep = pl.pallas_call(
        keep_kernel,
        out_shape=shape((TILE, CORE_ROWS, WIDTH), F32),
        in_specs=[VMEM, VMEM],
        out_specs=VMEM,
        scratch_shapes=[left],
        compiler_params=params(),
        name="keep_rows",
        cost_estimate=pl.CostEstimate(flops=1 << 29, bytes_accessed=8 << 20, transcendentals=0),
    )(amp, ints)
    own, one, two, three = pl.pallas_call(
        chip_kernel,
        out_shape=[shape((TILE, SLOTS, WIDTH), F32)] + [shape((SLOTS, MESSAGE), I32)] * 3,
        in_specs=[VMEM, VMEM],
        out_specs=[VMEM] * 4,
        scratch_shapes=[table, pltpu.VMEM((CORE_ROWS, MESSAGE), I32)],
        compiler_params=params(),
        name="chip_sum",
    )(keep, got)
    hops = [
        lax.ppermute(part, "pair", [(i, (i + CORES * hop) % OWNERS) for i in range(OWNERS)])
        for hop, part in ((1, one), (2, two), (3, three))
    ]
    parts = pl.pallas_call(
        column_kernel,
        out_shape=shape((COLUMNS, 16, 128), I32),
        in_specs=[VMEM] * 4,
        out_specs=VMEM,
        scratch_shapes=[pltpu.VMEM((TILE, SLOTS, WIDTH), F32), pltpu.VMEM((SLOTS, MESSAGE), I32)],
        compiler_params=params(),
        name="column_sum",
    )(own, *hops)
    back = lax.all_to_all(parts, "virt", split_axis=0, concat_axis=0, tiled=True)
    return pl.pallas_call(
        final_kernel,
        out_shape=shape((OWN_A, TILE, ROWS), F32),
        in_specs=[SMEM, SMEM, SMEM, VMEM, VMEM],
        out_specs=VMEM,
        scratch_shapes=[pltpu.VMEM((SLOTS, TILE * OWN_A), F32)],
        compiler_params=params(),
        name="unpack",
    )(number, virt, tile, pair_row, back)


def body(amplitudes, integrals, virt_irrep, tile_irrep, pair_irrep):
    run = functools.partial(
        one_round,
        amplitudes=amplitudes,
        integrals=integrals,
        virt=virt_irrep,
        tile=tile_irrep,
        pairs=pair_irrep,
    )
    counts = jnp.sum(
        (pair_irrep.reshape(OWNERS, ROWS)[:, :, None] == jnp.arange(8)).astype(I32), axis=1
    )
    rounds = (jnp.max(counts) + SLOTS - 1) // SLOTS
    first = run(jnp.zeros((), I32))
    _, total = lax.while_loop(
        lambda state: state[0] < rounds,
        lambda state: (state[0] + 1, state[1] + run(state[0])),
        (jnp.ones((), I32), first),
    )
    return jnp.transpose(total, (2, 1, 0))


def solution(mesh):
    in_specs = (P("pair", "virt", None), P("virt", "pair", None, None), P(), P(), P())
    out_specs = P("pair", None, "virt")
    return jax.shard_map(body, mesh=mesh, in_specs=in_specs, out_specs=out_specs, check_vma=False)
```

```python
import functools

import jax
import jax.numpy as jnp
from jax import lax
from jax.experimental import pallas as pl
from jax.experimental.pallas import tpu as pltpu
from jax.sharding import PartitionSpec as P

F32 = jnp.float32
BF16 = jnp.bfloat16
I32 = jnp.int32
SLOTS = 24
CHIPS = 4
CORES = 2
OWNERS = CHIPS * CORES
COLUMNS = 32
ROWS = 80
OWN_C = 10
OWN_D = 40
OWN_A = 10
TILE = 16
HALF = TILE // 2
WIDTH = 320
DEPTH = OWN_C * OWN_D
DEPTH_PAD = 512
WORDS = HALF * WIDTH
MESSAGE = WORDS + 128
CORE_ROWS = CHIPS * SLOTS
HOPS = (2, 1, 3, 0)
REST = CORE_ROWS - SLOTS
FINE = 64.0
FULL = 32767.0
WIDTH_PAD = 384
GROUPS = 2 * OWN_D // 16
PAIRS_B = TILE // 2
PAIR = 2 * WIDTH
NEAR = 6
FAR = PAIRS_B - NEAR
HBM = pl.BlockSpec(memory_space=pltpu.HBM)
VMEM = pl.BlockSpec(memory_space=pltpu.VMEM)
SMEM = pl.BlockSpec(memory_space=pltpu.SMEM)


def params():
    return pltpu.CompilerParams(vmem_limit_bytes=40 * 1024 * 1024)


def iota(shape, axis):
    return lax.broadcasted_iota(I32, shape, axis)


def local_labels(pairs_ref):
    owner = lax.axis_index("pair")
    every = pairs_ref[...].reshape(1, OWNERS * ROWS)
    row = every[:, 0:ROWS]
    for k in range(1, OWNERS):
        row = jnp.where(owner == k, every[:, k * ROWS : (k + 1) * ROWS], row)
    return row


def slots_of(row, round_index):
    first, second = iota((ROWS, ROWS), 0), iota((ROWS, ROWS), 1)
    spread = jnp.broadcast_to(row.astype(F32), (ROWS, ROWS))
    column = jnp.sum(jnp.where(first == second, spread, 0.0), axis=1, keepdims=True)
    before = (column == spread) & (first < second)
    rank = jnp.sum(jnp.where(before, 1.0, 0.0), axis=0, keepdims=True)
    slot = rank - (round_index * SLOTS).astype(F32)
    hot = iota((SLOTS, ROWS), 0).astype(F32) == slot
    return column, jnp.where(hot, 1.0, 0.0)


def pack_kernel(round_ref, virt_s, virt_v, pairs_v, amp_ref, out_ref, kept, wide):
    row = local_labels(pairs_v)
    column, hot = slots_of(row, round_ref[0])
    hot = hot.astype(BF16)
    column = column.astype(I32)
    base = lax.axis_index("virt") * OWN_C
    labels = virt_v[...].reshape(1, WIDTH)
    wide[:, :, 384:DEPTH_PAD] = jnp.zeros((OWNERS, SLOTS, DEPTH_PAD - 384), F32)
    for c in range(OWN_C):
        key = jnp.bitwise_xor(labels, virt_s[base + c])
        start = c * WIDTH_PAD
        kept[:, start : start + WIDTH] = jnp.where(column == key, amp_ref[c].astype(F32), 0.0).astype(BF16)
    packed = jnp.dot(hot, kept[...], preferred_element_type=F32)
    for c in range(OWN_C):
        for owner in range(OWNERS):
            start = c * WIDTH_PAD + owner * OWN_D
            wide[owner, :, c * OWN_D : (c + 1) * OWN_D] = packed[:, start : start + OWN_D]
    out_ref[...] = wide[...].astype(BF16)


def tile_column(tile_s):
    column = jnp.zeros((TILE, 1), I32)
    place = iota((TILE, 1), 0)
    for b in range(TILE):
        column = jnp.where(place == b, tile_s[b], column)
    return column


def mask_kernel(
    round_ref, virt_s, tile_s, virt_v, int_hbm, near_ref, far_hbm, slabs, masks, turn, wide, far, sems, far_sems
):
    del round_ref

    def load(c):
        return pltpu.make_async_copy(int_hbm.at[c], slabs.at[c], sems.at[c])

    def save(step):
        rows = pl.ds(pl.multiple_of(step * 2 * OWN_D, 16), 2 * OWN_D)
        return pltpu.make_async_copy(far.at[:, rows, :], far_hbm.at[:, rows, :], far_sems.at[step])

    for c in range(OWN_C):
        load(c).start()
    label = jnp.bitwise_xor(tile_column(tile_s), virt_v[...].reshape(1, WIDTH))
    for g in range(8):
        masks[g] = jnp.where(label == g, 1.0, 0.0).astype(BF16)
    high, low = iota((256, 256), 0), iota((256, 256), 1)
    match = (high // 16 == low % 16) & (high % 16 == low // 16)
    turn[...] = jnp.where(match, 1.0, 0.0).astype(BF16)
    base_c = lax.axis_index("virt") * OWN_C
    base_d = lax.axis_index("pair") * OWN_D

    @pl.loop(0, OWN_C // 2)
    def _(step):
        load(step * 2).wait()
        load(step * 2 + 1).wait()
        for group in range(GROUPS):
            for k in range(16):
                c, d = divmod(group * 16 + k, OWN_D)
                g = jnp.bitwise_xor(virt_s[base_c + step * 2 + c], virt_s[base_d + d])
                start = group * WIDTH_PAD
                wide[k * 16 : (k + 1) * 16, start : start + WIDTH] = slabs[step * 2 + c, d] * masks[g]
        turned = jnp.dot(turn[...], wide[...], preferred_element_type=F32).astype(BF16)
        for group in range(GROUPS):
            start = group * WIDTH_PAD
            rows = pl.ds(pl.multiple_of(step * 2 * OWN_D + group * 16, 16), 16)
            for b in range(TILE):
                pair, side = divmod(b, 2)
                out, at = (near_ref, pair) if pair < NEAR else (far, pair - NEAR)
                out[at, rows, side * WIDTH : (side + 1) * WIDTH] = turned[
                    b * 16 : (b + 1) * 16, start : start + WIDTH
                ]
        save(step).start()

    @pl.loop(0, OWN_C // 2)
    def _(step):
        save(step).wait()


def products(core, amp_ref, near_ref, far_hbm, left, far, sem, put):
    load = pltpu.make_async_copy(far_hbm, far, sem)
    load.start()
    x = lax.axis_index("pair") // CORES
    for at, hop in enumerate(HOPS):
        owner = lax.rem(x + hop, CHIPS) * CORES + core
        left[at * SLOTS : (at + 1) * SLOTS, :] = amp_ref[owner].astype(F32)
    rows = left[...].astype(BF16)[:, :DEPTH]
    for pair in range(NEAR):
        put(pair, jnp.dot(rows, near_ref[pair], preferred_element_type=F32))
    load.wait()
    for pair in range(FAR):
        put(NEAR + pair, jnp.dot(rows, far[pair], preferred_element_type=F32))


def scale_code(largest):
    return jnp.ceil(FINE * jnp.log2(jnp.maximum(largest, 1e-36))).astype(I32)


def scale_up(code):
    return FULL * jnp.exp2(code.astype(F32) * (-1.0 / FINE))


def scale_down(code):
    return jnp.exp2(code.astype(F32) * (1.0 / FINE)) * (1.0 / FULL)


def joined(high, low, factor):
    high = jnp.round(high * factor).astype(I32)
    low = jnp.round(low * factor).astype(I32)
    return jnp.left_shift(high, 16) | (low & 0xFFFF)


def high_of(word):
    return jnp.right_shift(word, 16).astype(F32)


def low_of(word):
    return jnp.right_shift(jnp.left_shift(word, 16), 16).astype(F32)


def row_largest(values):
    top = jnp.abs(values[0])
    for pair in range(1, PAIRS_B):
        top = jnp.maximum(top, jnp.abs(values[pair]))
    return jnp.max(top, axis=1, keepdims=True)


def write_words(values, outs):
    code = scale_code(row_largest(values))
    factor = scale_up(code)
    tail = jnp.broadcast_to(code, (code.shape[0], MESSAGE - WORDS))
    for pair in range(PAIRS_B // 2):
        words = joined(values[pair], values[pair + PAIRS_B // 2], factor)
        start = 0
        for out in outs:
            stop = start + out.shape[0]
            out[:, pair * PAIR : (pair + 1) * PAIR] = words[start:stop]
            start = stop
    start = 0
    for out in outs:
        stop = start + out.shape[0]
        out[:, WORDS:MESSAGE] = tail[start:stop]
        start = stop


def send_kernel(amp_ref, near_ref, far_hbm, far_out, rest_out, left, far, sem, values):
    def put(pair, value):
        values[pair] = value

    products(1 - lax.axis_index("pair") % CORES, amp_ref, near_ref, far_hbm, left, far, sem, put)
    write_words(values, (far_out, rest_out))


def keep_kernel(amp_ref, near_ref, far_hbm, far_out, rest_out, left, far, sem):
    def put(pair, value):
        far_out[pair] = value[0:SLOTS]
        rest_out[pair] = value[SLOTS:CORE_ROWS]

    products(lax.axis_index("pair") % CORES, amp_ref, near_ref, far_hbm, left, far, sem, put)


def add_words(words, values, start):
    factor = scale_down(words[:, WORDS : WORDS + 1])
    for pair in range(PAIRS_B // 2):
        word = words[:, pair * PAIR : (pair + 1) * PAIR]
        other = pair + PAIRS_B // 2
        values[pair] = start[pair] + high_of(word) * factor
        values[other] = start[other] + low_of(word) * factor


def two_kernel(keep_ref, got_ref, two_ref, values):
    add_words(got_ref, values, keep_ref)
    write_words(values, (two_ref,))


def near_kernel(keep_ref, got_ref, one_ref, three_ref, own_ref, values):
    add_words(got_ref, values, keep_ref)
    for pair in range(PAIRS_B):
        own_ref[pair] = values[pair, 2 * SLOTS : REST, :]
    write_words(values.at[:, 0 : 2 * SLOTS, :], (one_ref, three_ref))


def piece(group, b):
    index = group * HALF + b
    return 8 * (index // 12), OWN_A * (index % 12)


def column_kernel(own_ref, one_ref, two_ref, three_ref, out_ref, values, words):
    add_words(one_ref, values, own_ref)
    add_words(two_ref, values, values)
    add_words(three_ref, values, values)
    write_words(values, (words,))
    code = words[:, WORDS : WORDS + 8]
    lane = iota((8, 8), 1)
    tail = jnp.where(lane == 0, code[0:8], jnp.where(lane == 1, code[8:16], code[16:24]))
    for j in range(COLUMNS):
        for group in range(SLOTS // 8):
            for b in range(HALF):
                row, lane_at = piece(group, b)
                start = b * WIDTH + j * OWN_A
                out_ref[j, row : row + 8, lane_at : lane_at + OWN_A] = words[
                    group * 8 : group * 8 + 8, start : start + OWN_A
                ]
        out_ref[j, 0:8, 120:128] = tail
        out_ref[j, 8:16, 120:128] = tail


def final_kernel(round_ref, virt_s, tile_s, pairs_v, got_ref, out_ref, flat):
    row = local_labels(pairs_v)
    _, hot = slots_of(row, round_ref[0])
    lane = iota((8, 128), 1)
    sums = [[jnp.zeros((8, 128), F32) for _ in range(2)] for _ in range(2)]
    for j in range(COLUMNS):
        for block in range(2):
            word = got_ref[j, 8 * block : 8 * block + 8, :]
            if block == 0:
                code = jnp.where(lane < 80, word[:, 120:121], word[:, 121:122])
            else:
                code = jnp.where(lane < 40, word[:, 121:122], word[:, 122:123])
            factor = scale_down(code)
            sums[0][block] += high_of(word) * factor
            sums[1][block] += low_of(word) * factor
    for half in range(2):
        for group in range(SLOTS // 8):
            for b in range(HALF):
                at, lane_at = piece(group, b)
                to = (half * HALF + b) * OWN_A
                flat[group * 8 : group * 8 + 8, to : to + OWN_A] = sums[half][at // 8][:, lane_at : lane_at + OWN_A]
    spread = lax.dot_general(
        flat[...], hot, (((0,), (0,)), ((), ())), precision=lax.Precision.HIGHEST, preferred_element_type=F32
    )
    base = lax.axis_index("virt") * OWN_A
    column = tile_column(tile_s)
    for a in range(OWN_A):
        for b in range(TILE):
            out_ref[a, b : b + 1, :] = spread[b * OWN_A + a : b * OWN_A + a + 1]
        keep = jnp.bitwise_xor(column, virt_s[base + a]) == row
        out_ref[a] = jnp.where(keep, out_ref[a], 0.0)


def shape(dims, dtype):
    return jax.ShapeDtypeStruct(dims, dtype)


def masked_integrals(number, integrals, virt, tile):
    return pl.pallas_call(
        mask_kernel,
        out_shape=[pltpu.VMEM((NEAR, DEPTH, PAIR), BF16), pltpu.HBM((FAR, DEPTH, PAIR), BF16)],
        in_specs=[SMEM, SMEM, SMEM, VMEM, HBM],
        out_specs=[VMEM, HBM],
        scratch_shapes=[
            pltpu.VMEM((OWN_C, OWN_D, TILE, WIDTH), BF16),
            pltpu.VMEM((8, TILE, WIDTH), BF16),
            pltpu.VMEM((256, 256), BF16),
            pltpu.VMEM((256, GROUPS * WIDTH_PAD), BF16),
            pltpu.VMEM((FAR, DEPTH, PAIR), BF16),
            pltpu.SemaphoreType.DMA((OWN_C,)),
            pltpu.SemaphoreType.DMA((OWN_C // 2,)),
        ],
        compiler_params=params(),
        name="mask_turn",
        cost_estimate=pl.CostEstimate(flops=1 << 30, bytes_accessed=10 << 20, transcendentals=0),
    )(number, virt, tile, virt, pltpu.with_memory_space_constraint(integrals, pltpu.HBM))


def one_round(round_index, amplitudes, integrals, virt, tile, pairs):
    number = jnp.reshape(round_index, (1,)).astype(I32)
    packed = pl.pallas_call(
        pack_kernel,
        out_shape=shape((OWNERS, SLOTS, DEPTH_PAD), BF16),
        in_specs=[SMEM, SMEM, VMEM, VMEM, VMEM],
        out_specs=VMEM,
        scratch_shapes=[
            pltpu.VMEM((ROWS, OWN_C * WIDTH_PAD), BF16),
            pltpu.VMEM((OWNERS, SLOTS, DEPTH_PAD), F32),
        ],
        compiler_params=params(),
        name="pack",
    )(number, virt, virt, pairs, pltpu.with_memory_space_constraint(jnp.transpose(amplitudes, (1, 0, 2)), pltpu.HBM))
    amp = lax.all_to_all(packed, "pair", split_axis=0, concat_axis=0, tiled=True)
    near, far = masked_integrals(number, integrals, virt, tile)
    far = pltpu.with_memory_space_constraint(far, pltpu.HBM)
    left = pltpu.VMEM((CORE_ROWS, DEPTH_PAD), F32)
    table = pltpu.VMEM((PAIRS_B, CORE_ROWS, PAIR), F32)
    work = [left, pltpu.VMEM((FAR, DEPTH, PAIR), BF16), pltpu.SemaphoreType.DMA]
    message = shape((SLOTS, MESSAGE), I32)
    send = pl.pallas_call(
        send_kernel,
        out_shape=[message, shape((REST, MESSAGE), I32)],
        in_specs=[VMEM, VMEM, HBM],
        out_specs=[VMEM] * 2,
        scratch_shapes=[*work, table],
        compiler_params=params(),
        name="send_rows",
    )(amp, near, far)
    got = [lax.ppermute(part, "pair", [(i, i ^ 1) for i in range(OWNERS)]) for part in send]
    keep = pl.pallas_call(
        keep_kernel,
        out_shape=[shape((PAIRS_B, SLOTS, PAIR), F32), shape((PAIRS_B, REST, PAIR), F32)],
        in_specs=[VMEM, VMEM, HBM],
        out_specs=[VMEM] * 2,
        scratch_shapes=work,
        compiler_params=params(),
        name="keep_rows",
        cost_estimate=pl.CostEstimate(flops=1 << 29, bytes_accessed=8 << 20, transcendentals=0),
    )(amp, near, far)
    two = pl.pallas_call(
        two_kernel,
        out_shape=message,
        in_specs=[VMEM] * 2,
        out_specs=VMEM,
        scratch_shapes=[pltpu.VMEM((PAIRS_B, SLOTS, PAIR), F32)],
        compiler_params=params(),
        name="chip_sum_two",
    )(keep[0], got[0])
    one, three, own = pl.pallas_call(
        near_kernel,
        out_shape=[message, message, shape((PAIRS_B, SLOTS, PAIR), F32)],
        in_specs=[VMEM] * 2,
        out_specs=[VMEM] * 3,
        scratch_shapes=[pltpu.VMEM((PAIRS_B, REST, PAIR), F32)],
        compiler_params=params(),
        name="chip_sum_near",
    )(keep[1], got[1])
    hops = [
        lax.ppermute(part, "pair", [(i, (i + CORES * hop) % OWNERS) for i in range(OWNERS)])
        for hop, part in ((2, two), (1, one), (3, three))
    ]
    parts = pl.pallas_call(
        column_kernel,
        out_shape=shape((COLUMNS, 16, 128), I32),
        in_specs=[VMEM] * 4,
        out_specs=VMEM,
        scratch_shapes=[pltpu.VMEM((PAIRS_B, SLOTS, PAIR), F32), pltpu.VMEM((SLOTS, MESSAGE), I32)],
        compiler_params=params(),
        name="column_sum",
    )(own, *hops)
    back = lax.all_to_all(parts, "virt", split_axis=0, concat_axis=0, tiled=True)
    return pl.pallas_call(
        final_kernel,
        out_shape=pltpu.HBM((OWN_A, TILE, ROWS), F32),
        in_specs=[SMEM, SMEM, SMEM, VMEM, VMEM],
        out_specs=VMEM,
        scratch_shapes=[pltpu.VMEM((SLOTS, TILE * OWN_A), F32)],
        compiler_params=params(),
        name="unpack",
    )(number, virt, tile, pairs, back)


def body(amplitudes, integrals, virt_irrep, tile_irrep, pair_irrep):
    run = functools.partial(
        one_round,
        amplitudes=amplitudes,
        integrals=integrals,
        virt=virt_irrep,
        tile=tile_irrep,
        pairs=pair_irrep,
    )
    counts = jnp.sum(
        (pair_irrep.reshape(OWNERS, ROWS)[:, :, None] == jnp.arange(8)).astype(I32), axis=1
    )
    rounds = (jnp.max(counts) + SLOTS - 1) // SLOTS
    first = run(jnp.zeros((), I32))
    _, total = lax.while_loop(
        lambda state: state[0] < rounds,
        lambda state: (state[0] + 1, state[1] + run(state[0])),
        (jnp.ones((), I32), first),
    )
    return jnp.transpose(total, (2, 1, 0))


def solution(mesh):
    in_specs = (P("pair", "virt", None), P("virt", "pair", None, None), P(), P(), P())
    out_specs = P("pair", None, "virt")
    return jax.shard_map(body, mesh=mesh, in_specs=in_specs, out_specs=out_specs, check_vma=False)
```

```python
import functools

import jax
import jax.numpy as jnp
from jax import lax
from jax.experimental import pallas as pl
from jax.experimental.pallas import tpu as pltpu
from jax.sharding import PartitionSpec as P

F32 = jnp.float32
BF16 = jnp.bfloat16
I32 = jnp.int32
SLOTS = 24
CHIPS = 4
CORES = 2
OWNERS = CHIPS * CORES
COLUMNS = 32
ROWS = 80
OWN_C = 10
OWN_D = 40
OWN_A = 10
TILE = 16
HALF = TILE // 2
WIDTH = 320
DEPTH = OWN_C * OWN_D
DEPTH_PAD = 512
WORDS = HALF * WIDTH
MESSAGE = WORDS + 128
CORE_ROWS = CHIPS * SLOTS
LAYERS = 8
TILES = WORDS // 128
BLOCK = (TILES + 1) * SLOTS
FINE = 64.0
FULL = 32767.0
WIDTH_PAD = 384
GROUPS = 2 * OWN_D // 16
PAIRS_B = TILE // 2
PAIR = 2 * WIDTH
NEAR = 6
FAR = PAIRS_B - NEAR
HBM = pl.BlockSpec(memory_space=pltpu.HBM)
VMEM = pl.BlockSpec(memory_space=pltpu.VMEM)
SMEM = pl.BlockSpec(memory_space=pltpu.SMEM)


def params():
    return pltpu.CompilerParams(vmem_limit_bytes=40 * 1024 * 1024)


def iota(shape, axis):
    return lax.broadcasted_iota(I32, shape, axis)


def local_labels(pairs_ref):
    owner = lax.axis_index("pair")
    every = pairs_ref[...].reshape(1, OWNERS * ROWS)
    row = every[:, 0:ROWS]
    for k in range(1, OWNERS):
        row = jnp.where(owner == k, every[:, k * ROWS : (k + 1) * ROWS], row)
    return row


def slots_of(row, round_index):
    first, second = iota((ROWS, ROWS), 0), iota((ROWS, ROWS), 1)
    spread = jnp.broadcast_to(row.astype(F32), (ROWS, ROWS))
    column = jnp.sum(jnp.where(first == second, spread, 0.0), axis=1, keepdims=True)
    before = (column == spread) & (first < second)
    rank = jnp.sum(jnp.where(before, 1.0, 0.0), axis=0, keepdims=True)
    slot = rank - (round_index * SLOTS).astype(F32)
    hot = iota((SLOTS, ROWS), 0).astype(F32) == slot
    return column, jnp.where(hot, 1.0, 0.0)


def pack_kernel(round_ref, virt_s, virt_v, pairs_v, amp_ref, out_ref, kept, wide):
    row = local_labels(pairs_v)
    column, hot = slots_of(row, round_ref[0])
    hot = hot.astype(BF16)
    column = column.astype(I32)
    base = lax.axis_index("virt") * OWN_C
    labels = virt_v[...].reshape(1, WIDTH)
    wide[:, :, 384:DEPTH_PAD] = jnp.zeros((OWNERS, SLOTS, DEPTH_PAD - 384), F32)
    for c in range(OWN_C):
        key = jnp.bitwise_xor(labels, virt_s[base + c])
        start = c * WIDTH_PAD
        kept[:, start : start + WIDTH] = jnp.where(column == key, amp_ref[c].astype(F32), 0.0).astype(BF16)
    packed = jnp.dot(hot, kept[...], preferred_element_type=F32)
    for c in range(OWN_C):
        for owner in range(OWNERS):
            start = c * WIDTH_PAD + owner * OWN_D
            wide[owner, :, c * OWN_D : (c + 1) * OWN_D] = packed[:, start : start + OWN_D]
    out_ref[...] = wide[...].astype(BF16)


def tile_column(tile_s):
    column = jnp.zeros((TILE, 1), I32)
    place = iota((TILE, 1), 0)
    for b in range(TILE):
        column = jnp.where(place == b, tile_s[b], column)
    return column


def mask_kernel(
    round_ref, virt_s, tile_s, virt_v, int_hbm, near_ref, far_hbm, slabs, masks, turn, wide, far, sems, far_sems
):
    del round_ref

    def load(c):
        return pltpu.make_async_copy(int_hbm.at[c], slabs.at[c], sems.at[c])

    def save(step):
        rows = pl.ds(pl.multiple_of(step * 2 * OWN_D, 16), 2 * OWN_D)
        return pltpu.make_async_copy(far.at[:, rows, :], far_hbm.at[:, rows, :], far_sems.at[step])

    for c in range(OWN_C):
        load(c).start()
    label = jnp.bitwise_xor(tile_column(tile_s), virt_v[...].reshape(1, WIDTH))
    for g in range(8):
        masks[g] = jnp.where(label == g, 1.0, 0.0).astype(BF16)
    high, low = iota((256, 256), 0), iota((256, 256), 1)
    match = (high // 16 == low % 16) & (high % 16 == low // 16)
    turn[...] = jnp.where(match, 1.0, 0.0).astype(BF16)
    base_c = lax.axis_index("virt") * OWN_C
    base_d = lax.axis_index("pair") * OWN_D

    @pl.loop(0, OWN_C // 2)
    def _(step):
        load(step * 2).wait()
        load(step * 2 + 1).wait()
        for group in range(GROUPS):
            for k in range(16):
                c, d = divmod(group * 16 + k, OWN_D)
                g = jnp.bitwise_xor(virt_s[base_c + step * 2 + c], virt_s[base_d + d])
                start = group * WIDTH_PAD
                wide[k * 16 : (k + 1) * 16, start : start + WIDTH] = slabs[step * 2 + c, d] * masks[g]
        turned = jnp.dot(turn[...], wide[...], preferred_element_type=F32).astype(BF16)
        for group in range(GROUPS):
            start = group * WIDTH_PAD
            rows = pl.ds(pl.multiple_of(step * 2 * OWN_D + group * 16, 16), 16)
            for b in range(TILE):
                pair, side = divmod(b, 2)
                out, at = (near_ref, pair) if pair < NEAR else (far, pair - NEAR)
                out[at, rows, side * WIDTH : (side + 1) * WIDTH] = turned[
                    b * 16 : (b + 1) * 16, start : start + WIDTH
                ]
        save(step).start()

    @pl.loop(0, OWN_C // 2)
    def _(step):
        save(step).wait()


def products(core, amp_ref, near_ref, far_hbm, left, far, sem, put):
    load = pltpu.make_async_copy(far_hbm, far, sem)
    load.start()
    x = lax.axis_index("pair") // CORES
    for at in range(CHIPS):
        owner = jnp.where(core == 0, lax.rem(x + at, CHIPS), at) * CORES + core
        left[at * SLOTS : (at + 1) * SLOTS, :] = amp_ref[owner].astype(F32)
    rows = left[...].astype(BF16)[:, :DEPTH]
    for pair in range(NEAR):
        put(pair, jnp.dot(rows, near_ref[pair], preferred_element_type=F32))
    load.wait()
    for pair in range(FAR):
        put(NEAR + pair, jnp.dot(rows, far[pair], preferred_element_type=F32))


def scale_code(largest):
    return jnp.ceil(FINE * jnp.log2(jnp.maximum(largest, 1e-36))).astype(I32)


def scale_up(code):
    return FULL * jnp.exp2(code.astype(F32) * (-1.0 / FINE))


def scale_down(code):
    return jnp.exp2(code.astype(F32) * (1.0 / FINE)) * (1.0 / FULL)


def joined(high, low, factor):
    high = jnp.round(high * factor).astype(I32)
    low = jnp.round(low * factor).astype(I32)
    return jnp.left_shift(high, 16) | (low & 0xFFFF)


def high_of(word):
    return jnp.right_shift(word, 16).astype(F32)


def low_of(word):
    return jnp.right_shift(jnp.left_shift(word, 16), 16).astype(F32)


def row_largest(values):
    top = jnp.abs(values[0])
    for pair in range(1, PAIRS_B):
        top = jnp.maximum(top, jnp.abs(values[pair]))
    return jnp.max(top, axis=1, keepdims=True)


def write_words(values, out_ref):
    code = scale_code(row_largest(values))
    factor = scale_up(code)
    for pair in range(PAIRS_B // 2):
        out_ref[:, pair * PAIR : (pair + 1) * PAIR] = joined(values[pair], values[pair + PAIRS_B // 2], factor)
    out_ref[:, WORDS:MESSAGE] = jnp.broadcast_to(code, (code.shape[0], MESSAGE - WORDS))


def send_kernel(amp_ref, near_ref, far_hbm, out_ref, left, far, sem, values):
    def put(pair, value):
        values[pair] = value

    products(1 - lax.axis_index("pair") % CORES, amp_ref, near_ref, far_hbm, left, far, sem, put)
    write_words(values, out_ref)


def keep_kernel(amp_ref, near_ref, far_hbm, out_ref, left, far, sem):
    def put(pair, value):
        out_ref[pair] = value

    products(lax.axis_index("pair") % CORES, amp_ref, near_ref, far_hbm, left, far, sem, put)


def add_words(words, values, start):
    factor = scale_down(words[:, WORDS : WORDS + 1])
    for pair in range(PAIRS_B // 2):
        word = words[:, pair * PAIR : (pair + 1) * PAIR]
        other = pair + PAIRS_B // 2
        values[pair] = start[pair] + high_of(word) * factor
        values[other] = start[other] + low_of(word) * factor


def crossing(start, length):
    cuts, at = [], 0
    while at < length:
        tile, lane = divmod(start + at, 128)
        size = min(length - at, 128 - lane)
        cuts.append((at, tile, lane, size))
        at += size
    return cuts


def chip_kernel(keep_ref, got_ref, own_ref, one_ref, two_ref, three_ref, values, words, spread):
    core = lax.axis_index("pair") % CORES
    outs = (own_ref, one_ref, two_ref, three_ref)
    add_words(got_ref, values, keep_ref)
    write_words(values, words)

    @pl.when(core == 0)
    def _():
        for hop, out in enumerate(outs):
            for tile in range(TILES + 1):
                out[tile * SLOTS : (tile + 1) * SLOTS, :] = words[
                    hop * SLOTS : (hop + 1) * SLOTS, tile * 128 : (tile + 1) * 128
                ]

    @pl.when(core == 1)
    def _():
        own_width = WIDTH // CHIPS
        lane = iota((SLOTS, 128), 1)
        codes = [words[q * SLOTS : (q + 1) * SLOTS, WORDS:MESSAGE] for q in range(CHIPS)]
        tail = jnp.where(lane == 0, codes[0], jnp.where(lane == 1, codes[1], jnp.where(lane == 2, codes[2], codes[3])))
        for y in range(CHIPS):
            for b in range(HALF):
                for at, tile, to, size in crossing(b * own_width, own_width):
                    start = b * WIDTH + y * own_width + at
                    spread[y, tile * CORE_ROWS : (tile + 1) * CORE_ROWS, to : to + size] = words[
                        :, start : start + size
                    ]
            spread[y, TILES * SLOTS : BLOCK, :] = tail
        here = lax.axis_index("virt") // LAYERS
        for hop, out in enumerate(outs):
            out[...] = spread[lax.rem(here + hop, CHIPS)]


def piece(group, b):
    index = group * HALF + b
    return 8 * (index // 12), OWN_A * (index % 12)


def column_kernel(own_ref, one_ref, two_ref, three_ref, out_ref, high, low, words):
    core = lax.axis_index("pair") % CORES
    parts = (own_ref, one_ref, two_ref, three_ref)
    factors = [[scale_down(part[TILES * SLOTS : BLOCK, q : q + 1]) for q in range(CHIPS)] for part in parts]
    tops = [None] * CHIPS
    for tile in range(TILES):
        q = tile % CHIPS
        rows = slice(tile * SLOTS, (tile + 1) * SLOTS)
        word = [part[rows, :] for part in parts]
        high[rows, :] = sum(high_of(w) * f[q] for w, f in zip(word, factors))
        low[rows, :] = sum(low_of(w) * f[q] for w, f in zip(word, factors))
        top = jnp.maximum(jnp.abs(high[rows, :]), jnp.abs(low[rows, :]))
        tops[q] = top if tops[q] is None else jnp.maximum(tops[q], top)
    tops = [jnp.max(top, axis=1, keepdims=True) for top in tops]
    every = functools.reduce(jnp.maximum, tops)
    codes = [scale_code(jnp.where(core == 0, every, top)) for top in tops]
    ups = [scale_up(code) for code in codes]
    for tile in range(TILES):
        rows = slice(tile * SLOTS, (tile + 1) * SLOTS)
        words[rows, :] = joined(high[rows, :], low[rows, :], ups[tile % CHIPS])
    lane = iota((8, 8), 1)
    tails = [jnp.where(lane == 0, code[0:8], jnp.where(lane == 1, code[8:16], code[16:24])) for code in codes]

    def message(j, tail, place):
        for group in range(SLOTS // 8):
            for b in range(HALF):
                row, lane_at = piece(group, b)
                start, base, pitch = place(b)
                for at, tile, lane, size in crossing(start, OWN_A):
                    source = base + tile * pitch + group * 8
                    out_ref[j, row : row + 8, lane_at + at : lane_at + at + size] = words[
                        source : source + 8, lane : lane + size
                    ]
        out_ref[j, 0:8, 120:128] = tail
        out_ref[j, 8:16, 120:128] = tail

    @pl.when(core == 0)
    def _():
        for j in range(COLUMNS):
            message(j, tails[0], lambda b: (b * WIDTH + j * OWN_A, 0, SLOTS))

    @pl.when(core == 1)
    def _():
        for x in range(CHIPS):
            for z in range(LAYERS):
                message(
                    x * LAYERS + z,
                    tails[x],
                    lambda b: (b * (WIDTH // CHIPS) + z * OWN_A, x * SLOTS, CORE_ROWS),
                )


def final_kernel(round_ref, virt_s, tile_s, pairs_v, got_ref, out_ref, flat):
    row = local_labels(pairs_v)
    _, hot = slots_of(row, round_ref[0])
    lane = iota((8, 128), 1)
    sums = [[jnp.zeros((8, 128), F32) for _ in range(2)] for _ in range(2)]
    for j in range(COLUMNS):
        for block in range(2):
            word = got_ref[j, 8 * block : 8 * block + 8, :]
            if block == 0:
                code = jnp.where(lane < 80, word[:, 120:121], word[:, 121:122])
            else:
                code = jnp.where(lane < 40, word[:, 121:122], word[:, 122:123])
            factor = scale_down(code)
            sums[0][block] += high_of(word) * factor
            sums[1][block] += low_of(word) * factor
    for half in range(2):
        for group in range(SLOTS // 8):
            for b in range(HALF):
                at, lane_at = piece(group, b)
                to = (half * HALF + b) * OWN_A
                flat[group * 8 : group * 8 + 8, to : to + OWN_A] = sums[half][at // 8][:, lane_at : lane_at + OWN_A]
    spread = lax.dot_general(
        flat[...], hot, (((0,), (0,)), ((), ())), precision=lax.Precision.HIGHEST, preferred_element_type=F32
    )
    base = lax.axis_index("virt") * OWN_A
    column = tile_column(tile_s)
    for a in range(OWN_A):
        for b in range(TILE):
            out_ref[a, b : b + 1, :] = spread[b * OWN_A + a : b * OWN_A + a + 1]
        keep = jnp.bitwise_xor(column, virt_s[base + a]) == row
        out_ref[a] = jnp.where(keep, out_ref[a], 0.0)


def device(x, core, y, z):
    return ((x * CORES + core) * CHIPS + y) * LAYERS + z


def hop_pairs(hop):
    pairs = []
    for x in range(CHIPS):
        for y in range(CHIPS):
            for z in range(LAYERS):
                pairs.append((device(x, 0, y, z), device((x + hop) % CHIPS, 0, y, z)))
                pairs.append((device(x, 1, y, z), device(x, 1, (y + hop) % CHIPS, z)))
    return pairs


def column_groups():
    along = [(k, z) for k in range(CHIPS) for z in range(LAYERS)]
    first = [[device(x, 0, y, z) for y, z in along] for x in range(CHIPS)]
    return first + [[device(x, 1, y, z) for x, z in along] for y in range(CHIPS)]


def shape(dims, dtype):
    return jax.ShapeDtypeStruct(dims, dtype)


def masked_integrals(number, integrals, virt, tile):
    return pl.pallas_call(
        mask_kernel,
        out_shape=[pltpu.VMEM((NEAR, DEPTH, PAIR), BF16), pltpu.HBM((FAR, DEPTH, PAIR), BF16)],
        in_specs=[SMEM, SMEM, SMEM, VMEM, HBM],
        out_specs=[VMEM, HBM],
        scratch_shapes=[
            pltpu.VMEM((OWN_C, OWN_D, TILE, WIDTH), BF16),
            pltpu.VMEM((8, TILE, WIDTH), BF16),
            pltpu.VMEM((256, 256), BF16),
            pltpu.VMEM((256, GROUPS * WIDTH_PAD), BF16),
            pltpu.VMEM((FAR, DEPTH, PAIR), BF16),
            pltpu.SemaphoreType.DMA((OWN_C,)),
            pltpu.SemaphoreType.DMA((OWN_C // 2,)),
        ],
        compiler_params=params(),
        name="mask_turn",
        cost_estimate=pl.CostEstimate(flops=1 << 30, bytes_accessed=10 << 20, transcendentals=0),
    )(number, virt, tile, virt, pltpu.with_memory_space_constraint(integrals, pltpu.HBM))


def one_round(round_index, amplitudes, integrals, virt, tile, pairs):
    number = jnp.reshape(round_index, (1,)).astype(I32)
    packed = pl.pallas_call(
        pack_kernel,
        out_shape=shape((OWNERS, SLOTS, DEPTH_PAD), BF16),
        in_specs=[SMEM, SMEM, VMEM, VMEM, VMEM],
        out_specs=VMEM,
        scratch_shapes=[
            pltpu.VMEM((ROWS, OWN_C * WIDTH_PAD), BF16),
            pltpu.VMEM((OWNERS, SLOTS, DEPTH_PAD), F32),
        ],
        compiler_params=params(),
        name="pack",
    )(number, virt, virt, pairs, pltpu.with_memory_space_constraint(jnp.transpose(amplitudes, (1, 0, 2)), pltpu.HBM))
    amp = lax.all_to_all(packed, "pair", split_axis=0, concat_axis=0, tiled=True)
    near, far = masked_integrals(number, integrals, virt, tile)
    far = pltpu.with_memory_space_constraint(far, pltpu.HBM)
    left = pltpu.VMEM((CORE_ROWS, DEPTH_PAD), F32)
    table = pltpu.VMEM((PAIRS_B, CORE_ROWS, PAIR), F32)
    work = [left, pltpu.VMEM((FAR, DEPTH, PAIR), BF16), pltpu.SemaphoreType.DMA]
    send = pl.pallas_call(
        send_kernel,
        out_shape=shape((CORE_ROWS, MESSAGE), I32),
        in_specs=[VMEM, VMEM, HBM],
        out_specs=VMEM,
        scratch_shapes=[*work, table],
        compiler_params=params(),
        name="send_rows",
    )(amp, near, far)
    got = lax.ppermute(send, "pair", [(i, i ^ 1) for i in range(OWNERS)])
    keep = pl.pallas_call(
        keep_kernel,
        out_shape=shape((PAIRS_B, CORE_ROWS, PAIR), F32),
        in_specs=[VMEM, VMEM, HBM],
        out_specs=VMEM,
        scratch_shapes=work,
        compiler_params=params(),
        name="keep_rows",
        cost_estimate=pl.CostEstimate(flops=1 << 29, bytes_accessed=8 << 20, transcendentals=0),
    )(amp, near, far)
    own, one, two, three = pl.pallas_call(
        chip_kernel,
        out_shape=[shape((BLOCK, 128), I32)] * 4,
        in_specs=[VMEM] * 2,
        out_specs=[VMEM] * 4,
        scratch_shapes=[
            table,
            pltpu.VMEM((CORE_ROWS, MESSAGE), I32),
            pltpu.VMEM((CHIPS, BLOCK, 128), I32),
        ],
        compiler_params=params(),
        name="chip_sum",
    )(keep, got)
    two, one, three = [
        lax.ppermute(part, ("pair", "virt"), hop_pairs(hop)) for hop, part in ((2, two), (1, one), (3, three))
    ]
    parts = pl.pallas_call(
        column_kernel,
        out_shape=shape((COLUMNS, 16, 128), I32),
        in_specs=[VMEM] * 4,
        out_specs=VMEM,
        scratch_shapes=[pltpu.VMEM((TILES * SLOTS, 128), t) for t in (F32, F32, I32)],
        compiler_params=params(),
        name="column_sum",
    )(own, one, two, three)
    back = lax.all_to_all(
        parts, ("pair", "virt"), split_axis=0, concat_axis=0, tiled=True, axis_index_groups=column_groups()
    )
    return pl.pallas_call(
        final_kernel,
        out_shape=pltpu.HBM((OWN_A, TILE, ROWS), F32),
        in_specs=[SMEM, SMEM, SMEM, VMEM, VMEM],
        out_specs=VMEM,
        scratch_shapes=[pltpu.VMEM((SLOTS, TILE * OWN_A), F32)],
        compiler_params=params(),
        name="unpack",
    )(number, virt, tile, pairs, back)


def body(amplitudes, integrals, virt_irrep, tile_irrep, pair_irrep):
    run = functools.partial(
        one_round,
        amplitudes=amplitudes,
        integrals=integrals,
        virt=virt_irrep,
        tile=tile_irrep,
        pairs=pair_irrep,
    )
    counts = jnp.sum(
        (pair_irrep.reshape(OWNERS, ROWS)[:, :, None] == jnp.arange(8)).astype(I32), axis=1
    )
    rounds = (jnp.max(counts) + SLOTS - 1) // SLOTS
    first = run(jnp.zeros((), I32))
    _, total = lax.while_loop(
        lambda state: state[0] < rounds,
        lambda state: (state[0] + 1, state[1] + run(state[0])),
        (jnp.ones((), I32), first),
    )
    return jnp.transpose(total, (2, 1, 0))


def solution(mesh):
    in_specs = (P("pair", "virt", None), P("virt", "pair", None, None), P(), P(), P())
    out_specs = P("pair", None, "virt")
    return jax.shard_map(body, mesh=mesh, in_specs=in_specs, out_specs=out_specs, check_vma=False)
```

```python
import functools

import jax
import jax.numpy as jnp
from jax import lax
from jax.experimental import pallas as pl
from jax.experimental.pallas import tpu as pltpu
from jax.sharding import PartitionSpec as P

F32 = jnp.float32
BF16 = jnp.bfloat16
I32 = jnp.int32
SLOTS = 24
CHIPS = 4
CORES = 2
OWNERS = CHIPS * CORES
COLUMNS = 32
ROWS = 80
OWN_C = 10
OWN_D = 40
OWN_A = 10
TILE = 16
HALF = TILE // 2
WIDTH = 320
DEPTH = OWN_C * OWN_D
DEPTH_PAD = 512
WORDS = HALF * WIDTH
MESSAGE = WORDS + 128
CORE_ROWS = CHIPS * SLOTS
LAYERS = 8
TILES = WORDS // 128
BLOCK = (TILES + 1) * SLOTS
FINE = 64.0
FULL = 32767.0
WIDTH_PAD = 384
GROUPS = 2 * OWN_D // 16
PAIRS_B = TILE // 2
PAIR = 2 * WIDTH
NEAR = 6
FAR = PAIRS_B - NEAR
HBM = pl.BlockSpec(memory_space=pltpu.HBM)
VMEM = pl.BlockSpec(memory_space=pltpu.VMEM)
SMEM = pl.BlockSpec(memory_space=pltpu.SMEM)


def params():
    return pltpu.CompilerParams(vmem_limit_bytes=40 * 1024 * 1024)


def iota(shape, axis):
    return lax.broadcasted_iota(I32, shape, axis)


def local_labels(pairs_ref):
    owner = lax.axis_index("pair")
    every = pairs_ref[...].reshape(1, OWNERS * ROWS)
    row = every[:, 0:ROWS]
    for k in range(1, OWNERS):
        row = jnp.where(owner == k, every[:, k * ROWS : (k + 1) * ROWS], row)
    return row


def slots_of(row, round_index):
    first, second = iota((ROWS, ROWS), 0), iota((ROWS, ROWS), 1)
    spread = jnp.broadcast_to(row.astype(F32), (ROWS, ROWS))
    column = jnp.sum(jnp.where(first == second, spread, 0.0), axis=1, keepdims=True)
    before = (column == spread) & (first < second)
    rank = jnp.sum(jnp.where(before, 1.0, 0.0), axis=0, keepdims=True)
    slot = rank - (round_index * SLOTS).astype(F32)
    hot = iota((SLOTS, ROWS), 0).astype(F32) == slot
    return column, jnp.where(hot, 1.0, 0.0)


def pack_kernel(round_ref, virt_s, virt_v, pairs_v, amp_ref, out_ref, kept, wide):
    row = local_labels(pairs_v)
    column, hot = slots_of(row, round_ref[0])
    hot = hot.astype(BF16)
    column = column.astype(I32)
    base = lax.axis_index("virt") * OWN_C
    labels = virt_v[...].reshape(1, WIDTH)
    wide[:, :, 384:DEPTH_PAD] = jnp.zeros((OWNERS, SLOTS, DEPTH_PAD - 384), F32)
    for c in range(OWN_C):
        key = jnp.bitwise_xor(labels, virt_s[base + c])
        start = c * WIDTH_PAD
        kept[:, start : start + WIDTH] = jnp.where(column == key, amp_ref[c].astype(F32), 0.0).astype(BF16)
    packed = jnp.dot(hot, kept[...], preferred_element_type=F32)
    for c in range(OWN_C):
        for owner in range(OWNERS):
            start = c * WIDTH_PAD + owner * OWN_D
            wide[owner, :, c * OWN_D : (c + 1) * OWN_D] = packed[:, start : start + OWN_D]
    out_ref[...] = wide[...].astype(BF16)


def tile_column(tile_s):
    column = jnp.zeros((TILE, 1), I32)
    place = iota((TILE, 1), 0)
    for b in range(TILE):
        column = jnp.where(place == b, tile_s[b], column)
    return column


def mask_kernel(
    round_ref,
    virt_s,
    tile_s,
    virt_v,
    pairs_v,
    int_hbm,
    near_ref,
    far_hbm,
    hot_ref,
    keep_ref,
    slabs,
    masks,
    turn,
    wide,
    far,
    sems,
    far_sems,
):

    def load(c):
        return pltpu.make_async_copy(int_hbm.at[c], slabs.at[c], sems.at[c])

    def save(step):
        rows = pl.ds(pl.multiple_of(step * 2 * OWN_D, 16), 2 * OWN_D)
        return pltpu.make_async_copy(far.at[:, rows, :], far_hbm.at[:, rows, :], far_sems.at[step])

    for c in range(OWN_C):
        load(c).start()
    row = local_labels(pairs_v)
    _, hot = slots_of(row, round_ref[0])
    hot_ref[...] = hot
    column = tile_column(tile_s)
    base_a = lax.axis_index("virt") * OWN_A
    for a in range(OWN_A):
        keep_ref[a] = jnp.where(jnp.bitwise_xor(column, virt_s[base_a + a]) == row, 1.0, 0.0)
    label = jnp.bitwise_xor(column, virt_v[...].reshape(1, WIDTH))
    for g in range(8):
        masks[g] = jnp.where(label == g, 1.0, 0.0).astype(BF16)
    high, low = iota((256, 256), 0), iota((256, 256), 1)
    match = (high // 16 == low % 16) & (high % 16 == low // 16)
    turn[...] = jnp.where(match, 1.0, 0.0).astype(BF16)
    base_c = lax.axis_index("virt") * OWN_C
    base_d = lax.axis_index("pair") * OWN_D

    @pl.loop(0, OWN_C // 2)
    def _(step):
        load(step * 2).wait()
        load(step * 2 + 1).wait()
        for group in range(GROUPS):
            for k in range(16):
                c, d = divmod(group * 16 + k, OWN_D)
                g = jnp.bitwise_xor(virt_s[base_c + step * 2 + c], virt_s[base_d + d])
                start = group * WIDTH_PAD
                wide[k * 16 : (k + 1) * 16, start : start + WIDTH] = slabs[step * 2 + c, d] * masks[g]
        turned = jnp.dot(turn[...], wide[...], preferred_element_type=F32).astype(BF16)
        for group in range(GROUPS):
            start = group * WIDTH_PAD
            rows = pl.ds(pl.multiple_of(step * 2 * OWN_D + group * 16, 16), 16)
            for b in range(TILE):
                pair, side = divmod(b, 2)
                out, at = (near_ref, pair) if pair < NEAR else (far, pair - NEAR)
                out[at, rows, side * WIDTH : (side + 1) * WIDTH] = turned[
                    b * 16 : (b + 1) * 16, start : start + WIDTH
                ]
        save(step).start()

    @pl.loop(0, OWN_C // 2)
    def _(step):
        save(step).wait()


def products(core, amp_ref, near_ref, far_hbm, left, far, sem, put):
    load = pltpu.make_async_copy(far_hbm, far, sem)
    load.start()
    x = lax.axis_index("pair") // CORES
    for at in range(CHIPS):
        owner = jnp.where(core == 0, lax.rem(x + at, CHIPS), at) * CORES + core
        left[at * SLOTS : (at + 1) * SLOTS, :] = amp_ref[owner].astype(F32)
    rows = left[...].astype(BF16)[:, :DEPTH]
    for pair in range(NEAR):
        put(pair, jnp.dot(rows, near_ref[pair], preferred_element_type=F32))
    load.wait()
    for pair in range(FAR):
        put(NEAR + pair, jnp.dot(rows, far[pair], preferred_element_type=F32))


def scale_code(largest):
    return jnp.ceil(FINE * jnp.log2(jnp.maximum(largest, 1e-36))).astype(I32)


def scale_up(code):
    return FULL * jnp.exp2(code.astype(F32) * (-1.0 / FINE))


def scale_down(code):
    return jnp.exp2(code.astype(F32) * (1.0 / FINE)) * (1.0 / FULL)


def joined(high, low, factor):
    high = jnp.round(high * factor).astype(I32)
    low = jnp.round(low * factor).astype(I32)
    return jnp.left_shift(high, 16) | (low & 0xFFFF)


def high_of(word):
    return jnp.right_shift(word, 16).astype(F32)


def low_of(word):
    return jnp.right_shift(jnp.left_shift(word, 16), 16).astype(F32)


def folded(value):
    value = jnp.abs(value)
    return functools.reduce(jnp.maximum, [value[:, at : at + 128] for at in range(0, PAIR, 128)])


def write_words(values, top, out_ref):
    code = scale_code(jnp.max(top, axis=1, keepdims=True))
    factor = scale_up(code)
    for pair in range(PAIRS_B // 2):
        out_ref[:, pair * PAIR : (pair + 1) * PAIR] = joined(values[pair], values[pair + PAIRS_B // 2], factor)
    out_ref[:, WORDS:MESSAGE] = jnp.broadcast_to(code, (code.shape[0], MESSAGE - WORDS))


def send_kernel(amp_ref, near_ref, far_hbm, out_ref, left, far, sem, values):
    tops = []

    def put(pair, value):
        values[pair] = value
        top = folded(value)
        tops.append(jnp.maximum(tops[-1], top) if tops else top)

    products(1 - lax.axis_index("pair") % CORES, amp_ref, near_ref, far_hbm, left, far, sem, put)
    write_words(values, tops[-1], out_ref)


def keep_kernel(amp_ref, near_ref, far_hbm, out_ref, left, far, sem):
    def put(pair, value):
        out_ref[pair] = value

    products(lax.axis_index("pair") % CORES, amp_ref, near_ref, far_hbm, left, far, sem, put)


def add_words(words, values, start):
    top = None
    factor = scale_down(words[:, WORDS : WORDS + 1])
    for pair in range(PAIRS_B // 2):
        word = words[:, pair * PAIR : (pair + 1) * PAIR]
        other = pair + PAIRS_B // 2
        for at, part in ((pair, high_of(word)), (other, low_of(word))):
            value = start[at] + part * factor
            values[at] = value
            top = folded(value) if top is None else jnp.maximum(top, folded(value))
    return top


def crossing(start, length):
    cuts, at = [], 0
    while at < length:
        tile, lane = divmod(start + at, 128)
        size = min(length - at, 128 - lane)
        cuts.append((at, tile, lane, size))
        at += size
    return cuts


def chip_kernel(keep_ref, got_ref, own_ref, one_ref, three_ref, two_ref, values, words, spread):
    core = lax.axis_index("pair") % CORES
    outs = (own_ref, one_ref, two_ref, three_ref)
    top = add_words(got_ref, values, keep_ref)
    write_words(values, top, words)

    @pl.when(core == 0)
    def _():
        for hop, out in enumerate(outs):
            for tile in range(TILES + 1):
                out[tile * SLOTS : (tile + 1) * SLOTS, :] = words[
                    hop * SLOTS : (hop + 1) * SLOTS, tile * 128 : (tile + 1) * 128
                ]

    @pl.when(core == 1)
    def _():
        own_width = WIDTH // CHIPS
        lane = iota((SLOTS, 128), 1)
        codes = [words[q * SLOTS : (q + 1) * SLOTS, WORDS:MESSAGE] for q in range(CHIPS)]
        tail = jnp.where(lane == 0, codes[0], jnp.where(lane == 1, codes[1], jnp.where(lane == 2, codes[2], codes[3])))
        for y in range(CHIPS):
            for b in range(HALF):
                for at, tile, to, size in crossing(b * own_width, own_width):
                    start = b * WIDTH + y * own_width + at
                    spread[y, tile * CORE_ROWS : (tile + 1) * CORE_ROWS, to : to + size] = words[
                        :, start : start + size
                    ]
            spread[y, TILES * SLOTS : BLOCK, :] = tail
        here = lax.axis_index("virt") // LAYERS
        for hop, out in enumerate(outs):
            out[...] = spread[lax.rem(here + hop, CHIPS)]


def piece(group, b):
    index = group * HALF + b
    return 8 * (index // 12), OWN_A * (index % 12)


def column_kernel(own_ref, one_ref, three_ref, two_ref, out_ref, high, low, words):
    core = lax.axis_index("pair") % CORES
    parts = (own_ref, one_ref, two_ref, three_ref)
    factors = [[scale_down(part[TILES * SLOTS : BLOCK, q : q + 1]) for q in range(CHIPS)] for part in parts]
    tops = [None] * CHIPS
    for tile in range(TILES):
        q = tile % CHIPS
        rows = slice(tile * SLOTS, (tile + 1) * SLOTS)
        word = [part[rows, :] for part in parts]
        high[rows, :] = sum(high_of(w) * f[q] for w, f in zip(word, factors))
        low[rows, :] = sum(low_of(w) * f[q] for w, f in zip(word, factors))
        top = jnp.maximum(jnp.abs(high[rows, :]), jnp.abs(low[rows, :]))
        tops[q] = top if tops[q] is None else jnp.maximum(tops[q], top)
    tops = [jnp.max(top, axis=1, keepdims=True) for top in tops]
    every = functools.reduce(jnp.maximum, tops)
    codes = [scale_code(jnp.where(core == 0, every, top)) for top in tops]
    ups = [scale_up(code) for code in codes]
    for tile in range(TILES):
        rows = slice(tile * SLOTS, (tile + 1) * SLOTS)
        words[rows, :] = joined(high[rows, :], low[rows, :], ups[tile % CHIPS])
    lane = iota((8, 8), 1)
    tails = [jnp.where(lane == 0, code[0:8], jnp.where(lane == 1, code[8:16], code[16:24])) for code in codes]

    def message(j, tail, place):
        for group in range(SLOTS // 8):
            for b in range(HALF):
                row, lane_at = piece(group, b)
                start, base, pitch = place(b)
                for at, tile, lane, size in crossing(start, OWN_A):
                    source = base + tile * pitch + group * 8
                    out_ref[j, row : row + 8, lane_at + at : lane_at + at + size] = words[
                        source : source + 8, lane : lane + size
                    ]
        out_ref[j, 0:8, 120:128] = tail
        out_ref[j, 8:16, 120:128] = tail

    @pl.when(core == 0)
    def _():
        for j in range(COLUMNS):
            message(j, tails[0], lambda b: (b * WIDTH + j * OWN_A, 0, SLOTS))

    @pl.when(core == 1)
    def _():
        for x in range(CHIPS):
            for z in range(LAYERS):
                message(
                    x * LAYERS + z,
                    tails[x],
                    lambda b: (b * (WIDTH // CHIPS) + z * OWN_A, x * SLOTS, CORE_ROWS),
                )


def final_kernel(hot_ref, keep_ref, got_ref, out_ref, flat):
    lane = iota((8, 128), 1)
    sums = [[jnp.zeros((8, 128), F32) for _ in range(2)] for _ in range(2)]
    for j in range(COLUMNS):
        for block in range(2):
            word = got_ref[j, 8 * block : 8 * block + 8, :]
            if block == 0:
                code = jnp.where(lane < 80, word[:, 120:121], word[:, 121:122])
            else:
                code = jnp.where(lane < 40, word[:, 121:122], word[:, 122:123])
            factor = scale_down(code)
            sums[0][block] += high_of(word) * factor
            sums[1][block] += low_of(word) * factor
    for half in range(2):
        for group in range(SLOTS // 8):
            for b in range(HALF):
                at, lane_at = piece(group, b)
                to = (half * HALF + b) * OWN_A
                flat[group * 8 : group * 8 + 8, to : to + OWN_A] = sums[half][at // 8][:, lane_at : lane_at + OWN_A]
    spread = lax.dot_general(
        flat[...], hot_ref[...], (((0,), (0,)), ((), ())), precision=lax.Precision.HIGHEST, preferred_element_type=F32
    )
    for a in range(OWN_A):
        for b in range(TILE):
            out_ref[a, b : b + 1, :] = spread[b * OWN_A + a : b * OWN_A + a + 1]
        out_ref[a] = jnp.where(keep_ref[a] > 0.0, out_ref[a], 0.0)


def device(x, core, y, z):
    return ((x * CORES + core) * CHIPS + y) * LAYERS + z


def hop_pairs(hop):
    pairs = []
    for x in range(CHIPS):
        for y in range(CHIPS):
            for z in range(LAYERS):
                pairs.append((device(x, 0, y, z), device((x + hop) % CHIPS, 0, y, z)))
                pairs.append((device(x, 1, y, z), device(x, 1, (y + hop) % CHIPS, z)))
    return pairs


def column_groups():
    along = [(k, z) for k in range(CHIPS) for z in range(LAYERS)]
    first = [[device(x, 0, y, z) for y, z in along] for x in range(CHIPS)]
    return first + [[device(x, 1, y, z) for x, z in along] for y in range(CHIPS)]


def shape(dims, dtype):
    return jax.ShapeDtypeStruct(dims, dtype)


def masked_integrals(number, integrals, virt, tile, pairs):
    return pl.pallas_call(
        mask_kernel,
        out_shape=[
            pltpu.VMEM((NEAR, DEPTH, PAIR), BF16),
            pltpu.HBM((FAR, DEPTH, PAIR), BF16),
            shape((SLOTS, ROWS), F32),
            shape((OWN_A, TILE, ROWS), F32),
        ],
        in_specs=[SMEM, SMEM, SMEM, VMEM, VMEM, HBM],
        out_specs=[VMEM, HBM, VMEM, VMEM],
        scratch_shapes=[
            pltpu.VMEM((OWN_C, OWN_D, TILE, WIDTH), BF16),
            pltpu.VMEM((8, TILE, WIDTH), BF16),
            pltpu.VMEM((256, 256), BF16),
            pltpu.VMEM((256, GROUPS * WIDTH_PAD), BF16),
            pltpu.VMEM((FAR, DEPTH, PAIR), BF16),
            pltpu.SemaphoreType.DMA((OWN_C,)),
            pltpu.SemaphoreType.DMA((OWN_C // 2,)),
        ],
        compiler_params=params(),
        name="mask_turn",
        cost_estimate=pl.CostEstimate(flops=1 << 30, bytes_accessed=10 << 20, transcendentals=0),
    )(number, virt, tile, virt, pairs, pltpu.with_memory_space_constraint(integrals, pltpu.HBM))


def one_round(round_index, amplitudes, integrals, virt, tile, pairs):
    number = jnp.reshape(round_index, (1,)).astype(I32)
    packed = pl.pallas_call(
        pack_kernel,
        out_shape=shape((OWNERS, SLOTS, DEPTH_PAD), BF16),
        in_specs=[SMEM, SMEM, VMEM, VMEM, VMEM],
        out_specs=VMEM,
        scratch_shapes=[
            pltpu.VMEM((ROWS, OWN_C * WIDTH_PAD), BF16),
            pltpu.VMEM((OWNERS, SLOTS, DEPTH_PAD), F32),
        ],
        compiler_params=params(),
        name="pack",
    )(number, virt, virt, pairs, pltpu.with_memory_space_constraint(jnp.transpose(amplitudes, (1, 0, 2)), pltpu.HBM))
    amp = lax.all_to_all(packed, "pair", split_axis=0, concat_axis=0, tiled=True)
    near, far, hot, valid = masked_integrals(number, integrals, virt, tile, pairs)
    far = pltpu.with_memory_space_constraint(far, pltpu.HBM)
    left = pltpu.VMEM((CORE_ROWS, DEPTH_PAD), F32)
    table = pltpu.VMEM((PAIRS_B, CORE_ROWS, PAIR), F32)
    work = [left, pltpu.VMEM((FAR, DEPTH, PAIR), BF16), pltpu.SemaphoreType.DMA]
    send = pl.pallas_call(
        send_kernel,
        out_shape=shape((CORE_ROWS, MESSAGE), I32),
        in_specs=[VMEM, VMEM, HBM],
        out_specs=VMEM,
        scratch_shapes=[*work, table],
        compiler_params=params(),
        name="send_rows",
    )(amp, near, far)
    got = lax.ppermute(send, "pair", [(i, i ^ 1) for i in range(OWNERS)])
    keep = pl.pallas_call(
        keep_kernel,
        out_shape=shape((PAIRS_B, CORE_ROWS, PAIR), F32),
        in_specs=[VMEM, VMEM, HBM],
        out_specs=VMEM,
        scratch_shapes=work,
        compiler_params=params(),
        name="keep_rows",
        cost_estimate=pl.CostEstimate(flops=1 << 29, bytes_accessed=8 << 20, transcendentals=0),
    )(amp, near, far)
    own, one, three, two = pl.pallas_call(
        chip_kernel,
        out_shape=[shape((BLOCK, 128), I32)] * 4,
        in_specs=[VMEM] * 2,
        out_specs=[VMEM] * 4,
        scratch_shapes=[
            table,
            pltpu.VMEM((CORE_ROWS, MESSAGE), I32),
            pltpu.VMEM((CHIPS, BLOCK, 128), I32),
        ],
        compiler_params=params(),
        name="chip_sum",
    )(keep, got)
    one, three, two = [
        lax.ppermute(part, ("pair", "virt"), hop_pairs(hop)) for hop, part in ((1, one), (3, three), (2, two))
    ]
    parts = pl.pallas_call(
        column_kernel,
        out_shape=shape((COLUMNS, 16, 128), I32),
        in_specs=[VMEM] * 4,
        out_specs=VMEM,
        scratch_shapes=[pltpu.VMEM((TILES * SLOTS, 128), t) for t in (F32, F32, I32)],
        compiler_params=params(),
        name="column_sum",
    )(own, one, three, two)
    back = lax.all_to_all(
        parts, ("pair", "virt"), split_axis=0, concat_axis=0, tiled=True, axis_index_groups=column_groups()
    )
    return pl.pallas_call(
        final_kernel,
        out_shape=pltpu.HBM((OWN_A, TILE, ROWS), F32),
        in_specs=[VMEM] * 3,
        out_specs=VMEM,
        scratch_shapes=[pltpu.VMEM((SLOTS, TILE * OWN_A), F32)],
        compiler_params=params(),
        name="unpack",
    )(hot, valid, back)


def body(amplitudes, integrals, virt_irrep, tile_irrep, pair_irrep):
    run = functools.partial(
        one_round,
        amplitudes=amplitudes,
        integrals=integrals,
        virt=virt_irrep,
        tile=tile_irrep,
        pairs=pair_irrep,
    )
    counts = jnp.sum(
        (pair_irrep.reshape(OWNERS, ROWS)[:, :, None] == jnp.arange(8)).astype(I32), axis=1
    )
    rounds = (jnp.max(counts) + SLOTS - 1) // SLOTS
    first = run(jnp.zeros((), I32))
    _, total = lax.while_loop(
        lambda state: state[0] < rounds,
        lambda state: (state[0] + 1, state[1] + run(state[0])),
        (jnp.ones((), I32), first),
    )
    return jnp.transpose(total, (2, 1, 0))


def solution(mesh):
    in_specs = (P("pair", "virt", None), P("virt", "pair", None, None), P(), P(), P())
    out_specs = P("pair", None, "virt")
    return jax.shard_map(body, mesh=mesh, in_specs=in_specs, out_specs=out_specs, check_vma=False)
```

```python
import functools

import jax
import jax.numpy as jnp
from jax import lax
from jax.experimental import pallas as pl
from jax.experimental.pallas import tpu as pltpu
from jax.sharding import PartitionSpec as P

F32 = jnp.float32
BF16 = jnp.bfloat16
I32 = jnp.int32
SLOTS = 24
CHIPS = 4
CORES = 2
OWNERS = CHIPS * CORES
COLUMNS = 32
ROWS = 80
OWN_C = 10
OWN_D = 40
OWN_A = 10
TILE = 16
HALF = TILE // 2
WIDTH = 320
DEPTH = OWN_C * OWN_D
DEPTH_PAD = 512
WORDS = HALF * WIDTH
MESSAGE = WORDS + 128
CORE_ROWS = CHIPS * SLOTS
LAYERS = 8
TILES = WORDS // 128
BLOCK = (TILES + 1) * SLOTS
FINE = 64.0
FULL = 32767.0
WIDTH_PAD = 384
GROUPS = 2 * OWN_D // 16
PAIRS_B = TILE // 2
PAIR = 2 * WIDTH
NEAR = 6
FAR = PAIRS_B - NEAR
HBM = pl.BlockSpec(memory_space=pltpu.HBM)
VMEM = pl.BlockSpec(memory_space=pltpu.VMEM)
SMEM = pl.BlockSpec(memory_space=pltpu.SMEM)


def params():
    return pltpu.CompilerParams(vmem_limit_bytes=40 * 1024 * 1024)


def iota(shape, axis):
    return lax.broadcasted_iota(I32, shape, axis)


def local_labels(pairs_ref):
    owner = lax.axis_index("pair")
    every = pairs_ref[...].reshape(1, OWNERS * ROWS)
    row = every[:, 0:ROWS]
    for k in range(1, OWNERS):
        row = jnp.where(owner == k, every[:, k * ROWS : (k + 1) * ROWS], row)
    return row


def slots_of(row, round_index):
    first, second = iota((ROWS, ROWS), 0), iota((ROWS, ROWS), 1)
    spread = jnp.broadcast_to(row.astype(F32), (ROWS, ROWS))
    column = jnp.sum(jnp.where(first == second, spread, 0.0), axis=1, keepdims=True)
    before = (column == spread) & (first < second)
    rank = jnp.sum(jnp.where(before, 1.0, 0.0), axis=0, keepdims=True)
    slot = rank - (round_index * SLOTS).astype(F32)
    hot = iota((SLOTS, ROWS), 0).astype(F32) == slot
    return column, jnp.where(hot, 1.0, 0.0)


def pack_kernel(round_ref, virt_s, virt_v, pairs_v, amp_ref, out_ref, kept, wide):
    row = local_labels(pairs_v)
    column, hot = slots_of(row, round_ref[0])
    hot = hot.astype(BF16)
    column = column.astype(I32)
    base = lax.axis_index("virt") * OWN_C
    labels = virt_v[...].reshape(1, WIDTH)
    wide[:, :, 384:DEPTH_PAD] = jnp.zeros((OWNERS, SLOTS, DEPTH_PAD - 384), F32)
    for c in range(OWN_C):
        key = jnp.bitwise_xor(labels, virt_s[base + c])
        start = c * WIDTH_PAD
        kept[:, start : start + WIDTH] = jnp.where(column == key, amp_ref[c].astype(F32), 0.0).astype(BF16)
    packed = jnp.dot(hot, kept[...], preferred_element_type=F32)
    for c in range(OWN_C):
        for owner in range(OWNERS):
            start = c * WIDTH_PAD + owner * OWN_D
            wide[owner, :, c * OWN_D : (c + 1) * OWN_D] = packed[:, start : start + OWN_D]
    out_ref[...] = wide[...].astype(BF16)


def tile_column(tile_s):
    column = jnp.zeros((TILE, 1), I32)
    place = iota((TILE, 1), 0)
    for b in range(TILE):
        column = jnp.where(place == b, tile_s[b], column)
    return column


def mask_kernel(
    round_ref,
    virt_s,
    tile_s,
    virt_v,
    pairs_v,
    int_hbm,
    near_ref,
    far_hbm,
    hot_ref,
    keep_ref,
    slabs,
    masks,
    turn,
    wide,
    far,
    sems,
    far_sems,
):

    def load(c):
        return pltpu.make_async_copy(int_hbm.at[c], slabs.at[c], sems.at[c])

    def save(step):
        rows = pl.ds(step * 2 * OWN_D, 2 * OWN_D)
        return pltpu.make_async_copy(far.at[:, rows, :], far_hbm.at[:, rows, :], far_sems.at[step])

    for c in range(OWN_C):
        load(c).start()
    row = local_labels(pairs_v)
    _, hot = slots_of(row, round_ref[0])
    hot_ref[...] = hot
    column = tile_column(tile_s)
    base_a = lax.axis_index("virt") * OWN_A
    for a in range(OWN_A):
        keep_ref[a] = jnp.where(jnp.bitwise_xor(column, virt_s[base_a + a]) == row, 1.0, 0.0)
    label = jnp.bitwise_xor(column, virt_v[...].reshape(1, WIDTH))
    for g in range(8):
        masks[g] = jnp.where(label == g, 1.0, 0.0).astype(BF16)
    high, low = iota((256, 256), 0), iota((256, 256), 1)
    match = (high // 16 == low % 16) & (high % 16 == low // 16)
    turn[...] = jnp.where(match, 1.0, 0.0).astype(BF16)
    base_c = lax.axis_index("virt") * OWN_C
    base_d = lax.axis_index("pair") * OWN_D

    for step in range(OWN_C // 2):
        buffer = wide.at[step % 2]
        load(step * 2).wait()
        load(step * 2 + 1).wait()
        for group in range(GROUPS):
            for k in range(16):
                c, d = divmod(group * 16 + k, OWN_D)
                g = jnp.bitwise_xor(virt_s[base_c + step * 2 + c], virt_s[base_d + d])
                start = group * WIDTH_PAD
                buffer[k * 16 : (k + 1) * 16, start : start + WIDTH] = slabs[step * 2 + c, d] * masks[g]
        turned = jnp.dot(turn[...], buffer[...], preferred_element_type=F32).astype(BF16)
        for group in range(GROUPS):
            start = group * WIDTH_PAD
            rows = pl.ds(step * 2 * OWN_D + group * 16, 16)
            for b in range(TILE):
                pair, side = divmod(b, 2)
                out, at = (near_ref, pair) if pair < NEAR else (far, pair - NEAR)
                out[at, rows, side * WIDTH : (side + 1) * WIDTH] = turned[
                    b * 16 : (b + 1) * 16, start : start + WIDTH
                ]
        save(step).start()

    for step in range(OWN_C // 2):
        save(step).wait()


def products(core, amp_ref, near_ref, far_hbm, left, far, sem, put):
    load = pltpu.make_async_copy(far_hbm, far, sem)
    load.start()
    x = lax.axis_index("pair") // CORES
    for at in range(CHIPS):
        owner = jnp.where(core == 0, lax.rem(x + at, CHIPS), at) * CORES + core
        left[at * SLOTS : (at + 1) * SLOTS, :] = amp_ref[owner].astype(F32)
    rows = left[...].astype(BF16)[:, :DEPTH]
    for pair in range(NEAR):
        put(pair, jnp.dot(rows, near_ref[pair], preferred_element_type=F32))
    load.wait()
    for pair in range(FAR):
        put(NEAR + pair, jnp.dot(rows, far[pair], preferred_element_type=F32))


def scale_code(largest):
    return jnp.ceil(FINE * jnp.log2(jnp.maximum(largest, 1e-36))).astype(I32)


def scale_up(code):
    return FULL * jnp.exp2(code.astype(F32) * (-1.0 / FINE))


def scale_down(code):
    return jnp.exp2(code.astype(F32) * (1.0 / FINE)) * (1.0 / FULL)


def joined(high, low, factor):
    high = jnp.round(high * factor).astype(I32)
    low = jnp.round(low * factor).astype(I32)
    return jnp.left_shift(high, 16) | (low & 0xFFFF)


def high_of(word):
    return jnp.right_shift(word, 16).astype(F32)


def low_of(word):
    return jnp.right_shift(jnp.left_shift(word, 16), 16).astype(F32)


def folded(value):
    value = jnp.abs(value)
    return functools.reduce(jnp.maximum, [value[:, at : at + 128] for at in range(0, PAIR, 128)])


def write_words(values, top, out_ref):
    code = scale_code(jnp.max(top, axis=1, keepdims=True))
    factor = scale_up(code)
    for pair in range(PAIRS_B // 2):
        out_ref[:, pair * PAIR : (pair + 1) * PAIR] = joined(values[pair], values[pair + PAIRS_B // 2], factor)
    out_ref[:, WORDS:MESSAGE] = jnp.broadcast_to(code, (code.shape[0], MESSAGE - WORDS))


def send_kernel(amp_ref, near_ref, far_hbm, out_ref, left, far, sem, values):
    tops = []

    def put(pair, value):
        values[pair] = value
        top = folded(value)
        tops.append(jnp.maximum(tops[-1], top) if tops else top)

    products(1 - lax.axis_index("pair") % CORES, amp_ref, near_ref, far_hbm, left, far, sem, put)
    write_words(values, tops[-1], out_ref)


def keep_kernel(amp_ref, near_ref, far_hbm, out_ref, left, far, sem):
    def put(pair, value):
        out_ref[pair] = value

    products(lax.axis_index("pair") % CORES, amp_ref, near_ref, far_hbm, left, far, sem, put)


def add_words(words, values, start):
    top = None
    factor = scale_down(words[:, WORDS : WORDS + 1])
    for pair in range(PAIRS_B // 2):
        word = words[:, pair * PAIR : (pair + 1) * PAIR]
        other = pair + PAIRS_B // 2
        for at, part in ((pair, high_of(word)), (other, low_of(word))):
            value = start[at] + part * factor
            values[at] = value
            top = folded(value) if top is None else jnp.maximum(top, folded(value))
    return top


def crossing(start, length):
    cuts, at = [], 0
    while at < length:
        tile, lane = divmod(start + at, 128)
        size = min(length - at, 128 - lane)
        cuts.append((at, tile, lane, size))
        at += size
    return cuts


def chip_kernel(keep_ref, got_ref, own_ref, one_ref, three_ref, two_ref, values, words):
    core = lax.axis_index("pair") % CORES
    outs = (own_ref, one_ref, two_ref, three_ref)
    top = add_words(got_ref, values, keep_ref)
    write_words(values, top, words)

    @pl.when(core == 0)
    def _():
        for hop, out in enumerate(outs):
            for tile in range(TILES + 1):
                out[tile * SLOTS : (tile + 1) * SLOTS, :] = words[
                    hop * SLOTS : (hop + 1) * SLOTS, tile * 128 : (tile + 1) * 128
                ]

    @pl.when(core == 1)
    def _():
        own_width = WIDTH // CHIPS
        lane = iota((SLOTS, 128), 1)
        codes = [words[q * SLOTS : (q + 1) * SLOTS, WORDS:MESSAGE] for q in range(CHIPS)]
        tail = jnp.where(lane == 0, codes[0], jnp.where(lane == 1, codes[1], jnp.where(lane == 2, codes[2], codes[3])))
        here = lax.axis_index("virt") // LAYERS
        for y in range(CHIPS):

            @pl.when(here == y)
            def _():
                for hop, out in enumerate(outs):
                    for b in range(HALF):
                        for at, tile, to, size in crossing(b * own_width, own_width):
                            start = b * WIDTH + (y + hop) % CHIPS * own_width + at
                            out[tile * CORE_ROWS : (tile + 1) * CORE_ROWS, to : to + size] = words[
                                :, start : start + size
                            ]

        for out in outs:
            out[TILES * SLOTS : BLOCK, :] = tail


def piece(group, b):
    index = group * HALF + b
    return 8 * (index // 12), OWN_A * (index % 12)


def column_kernel(own_ref, one_ref, three_ref, two_ref, out_ref, high, low, words):
    core = lax.axis_index("pair") % CORES
    parts = (own_ref, one_ref, two_ref, three_ref)
    factors = [[scale_down(part[TILES * SLOTS : BLOCK, q : q + 1]) for q in range(CHIPS)] for part in parts]
    tops = [None] * CHIPS
    for tile in range(TILES):
        q = tile % CHIPS
        rows = slice(tile * SLOTS, (tile + 1) * SLOTS)
        word = [part[rows, :] for part in parts]
        high[rows, :] = sum(high_of(w) * f[q] for w, f in zip(word, factors))
        low[rows, :] = sum(low_of(w) * f[q] for w, f in zip(word, factors))
        top = jnp.maximum(jnp.abs(high[rows, :]), jnp.abs(low[rows, :]))
        tops[q] = top if tops[q] is None else jnp.maximum(tops[q], top)
    tops = [jnp.max(top, axis=1, keepdims=True) for top in tops]
    every = functools.reduce(jnp.maximum, tops)
    codes = [scale_code(jnp.where(core == 0, every, top)) for top in tops]
    ups = [scale_up(code) for code in codes]
    for tile in range(TILES):
        rows = slice(tile * SLOTS, (tile + 1) * SLOTS)
        words[rows, :] = joined(high[rows, :], low[rows, :], ups[tile % CHIPS])
    lane = iota((8, 8), 1)
    tails = [jnp.where(lane == 0, code[0:8], jnp.where(lane == 1, code[8:16], code[16:24])) for code in codes]

    def message(j, tail, place):
        for group in range(SLOTS // 8):
            for b in range(HALF):
                row, lane_at = piece(group, b)
                start, base, pitch = place(b)
                for at, tile, lane, size in crossing(start, OWN_A):
                    source = base + tile * pitch + group * 8
                    out_ref[j, row : row + 8, lane_at + at : lane_at + at + size] = words[
                        source : source + 8, lane : lane + size
                    ]
        out_ref[j, 0:8, 120:128] = tail
        out_ref[j, 8:16, 120:128] = tail

    @pl.when(core == 0)
    def _():
        for j in range(COLUMNS):
            message(j, tails[0], lambda b: (b * WIDTH + j * OWN_A, 0, SLOTS))

    @pl.when(core == 1)
    def _():
        for x in range(CHIPS):
            for z in range(LAYERS):
                message(
                    x * LAYERS + z,
                    tails[x],
                    lambda b: (b * (WIDTH // CHIPS) + z * OWN_A, x * SLOTS, CORE_ROWS),
                )


def final_kernel(hot_ref, keep_ref, got_ref, out_ref, flat):
    lane = iota((8, 128), 1)
    sums = [[jnp.zeros((8, 128), F32) for _ in range(2)] for _ in range(2)]
    for j in range(COLUMNS):
        for block in range(2):
            word = got_ref[j, 8 * block : 8 * block + 8, :]
            if block == 0:
                code = jnp.where(lane < 80, word[:, 120:121], word[:, 121:122])
            else:
                code = jnp.where(lane < 40, word[:, 121:122], word[:, 122:123])
            factor = scale_down(code)
            sums[0][block] += high_of(word) * factor
            sums[1][block] += low_of(word) * factor
    for half in range(2):
        for group in range(SLOTS // 8):
            for b in range(HALF):
                at, lane_at = piece(group, b)
                to = (half * HALF + b) * OWN_A
                flat[group * 8 : group * 8 + 8, to : to + OWN_A] = sums[half][at // 8][:, lane_at : lane_at + OWN_A]
    spread = lax.dot_general(
        flat[...], hot_ref[...], (((0,), (0,)), ((), ())), precision=lax.Precision.HIGHEST, preferred_element_type=F32
    )
    for a in range(OWN_A):
        for b in range(TILE):
            out_ref[a, b : b + 1, :] = spread[b * OWN_A + a : b * OWN_A + a + 1]
        out_ref[a] = jnp.where(keep_ref[a] > 0.0, out_ref[a], 0.0)


def device(x, core, y, z):
    return ((x * CORES + core) * CHIPS + y) * LAYERS + z


def hop_pairs(hop):
    pairs = []
    for x in range(CHIPS):
        for y in range(CHIPS):
            for z in range(LAYERS):
                pairs.append((device(x, 0, y, z), device((x + hop) % CHIPS, 0, y, z)))
                pairs.append((device(x, 1, y, z), device(x, 1, (y + hop) % CHIPS, z)))
    return pairs


def column_groups():
    along = [(k, z) for k in range(CHIPS) for z in range(LAYERS)]
    first = [[device(x, 0, y, z) for y, z in along] for x in range(CHIPS)]
    return first + [[device(x, 1, y, z) for x, z in along] for y in range(CHIPS)]


def shape(dims, dtype):
    return jax.ShapeDtypeStruct(dims, dtype)


def masked_integrals(number, integrals, virt, tile, pairs):
    return pl.pallas_call(
        mask_kernel,
        out_shape=[
            pltpu.VMEM((NEAR, DEPTH, PAIR), BF16),
            pltpu.HBM((FAR, DEPTH, PAIR), BF16),
            shape((SLOTS, ROWS), F32),
            shape((OWN_A, TILE, ROWS), F32),
        ],
        in_specs=[SMEM, SMEM, SMEM, VMEM, VMEM, HBM],
        out_specs=[VMEM, HBM, VMEM, VMEM],
        scratch_shapes=[
            pltpu.VMEM((OWN_C, OWN_D, TILE, WIDTH), BF16),
            pltpu.VMEM((8, TILE, WIDTH), BF16),
            pltpu.VMEM((256, 256), BF16),
            pltpu.VMEM((2, 256, GROUPS * WIDTH_PAD), BF16),
            pltpu.VMEM((FAR, DEPTH, PAIR), BF16),
            pltpu.SemaphoreType.DMA((OWN_C,)),
            pltpu.SemaphoreType.DMA((OWN_C // 2,)),
        ],
        compiler_params=params(),
        name="mask_turn",
        cost_estimate=pl.CostEstimate(flops=1 << 30, bytes_accessed=10 << 20, transcendentals=0),
    )(number, virt, tile, virt, pairs, pltpu.with_memory_space_constraint(integrals, pltpu.HBM))


def one_round(round_index, amplitudes, integrals, virt, tile, pairs):
    number = jnp.reshape(round_index, (1,)).astype(I32)
    packed = pl.pallas_call(
        pack_kernel,
        out_shape=shape((OWNERS, SLOTS, DEPTH_PAD), BF16),
        in_specs=[SMEM, SMEM, VMEM, VMEM, VMEM],
        out_specs=VMEM,
        scratch_shapes=[
            pltpu.VMEM((ROWS, OWN_C * WIDTH_PAD), BF16),
            pltpu.VMEM((OWNERS, SLOTS, DEPTH_PAD), F32),
        ],
        compiler_params=params(),
        name="pack",
    )(number, virt, virt, pairs, pltpu.with_memory_space_constraint(jnp.transpose(amplitudes, (1, 0, 2)), pltpu.HBM))
    amp = lax.all_to_all(packed, "pair", split_axis=0, concat_axis=0, tiled=True)
    near, far, hot, valid = masked_integrals(number, integrals, virt, tile, pairs)
    far = pltpu.with_memory_space_constraint(far, pltpu.HBM)
    left = pltpu.VMEM((CORE_ROWS, DEPTH_PAD), F32)
    table = pltpu.VMEM((PAIRS_B, CORE_ROWS, PAIR), F32)
    work = [left, pltpu.VMEM((FAR, DEPTH, PAIR), BF16), pltpu.SemaphoreType.DMA]
    send = pl.pallas_call(
        send_kernel,
        out_shape=shape((CORE_ROWS, MESSAGE), I32),
        in_specs=[VMEM, VMEM, HBM],
        out_specs=VMEM,
        scratch_shapes=[*work, table],
        compiler_params=params(),
        name="send_rows",
    )(amp, near, far)
    got = lax.ppermute(send, "pair", [(i, i ^ 1) for i in range(OWNERS)])
    keep = pl.pallas_call(
        keep_kernel,
        out_shape=shape((PAIRS_B, CORE_ROWS, PAIR), F32),
        in_specs=[VMEM, VMEM, HBM],
        out_specs=VMEM,
        scratch_shapes=work,
        compiler_params=params(),
        name="keep_rows",
        cost_estimate=pl.CostEstimate(flops=1 << 29, bytes_accessed=8 << 20, transcendentals=0),
    )(amp, near, far)
    own, one, three, two = pl.pallas_call(
        chip_kernel,
        out_shape=[shape((BLOCK, 128), I32)] * 4,
        in_specs=[VMEM] * 2,
        out_specs=[VMEM] * 4,
        scratch_shapes=[
            table,
            pltpu.VMEM((CORE_ROWS, MESSAGE), I32),
        ],
        compiler_params=params(),
        name="chip_sum",
    )(keep, got)
    one, three, two = [
        lax.ppermute(part, ("pair", "virt"), hop_pairs(hop)) for hop, part in ((1, one), (3, three), (2, two))
    ]
    parts = pl.pallas_call(
        column_kernel,
        out_shape=shape((COLUMNS, 16, 128), I32),
        in_specs=[VMEM] * 4,
        out_specs=VMEM,
        scratch_shapes=[pltpu.VMEM((TILES * SLOTS, 128), t) for t in (F32, F32, I32)],
        compiler_params=params(),
        name="column_sum",
    )(own, one, three, two)
    back = lax.all_to_all(
        parts, ("pair", "virt"), split_axis=0, concat_axis=0, tiled=True, axis_index_groups=column_groups()
    )
    return pl.pallas_call(
        final_kernel,
        out_shape=pltpu.HBM((OWN_A, TILE, ROWS), F32),
        in_specs=[VMEM] * 3,
        out_specs=VMEM,
        scratch_shapes=[pltpu.VMEM((SLOTS, TILE * OWN_A), F32)],
        compiler_params=params(),
        name="unpack",
    )(hot, valid, back)


def body(amplitudes, integrals, virt_irrep, tile_irrep, pair_irrep):
    run = functools.partial(
        one_round,
        amplitudes=amplitudes,
        integrals=integrals,
        virt=virt_irrep,
        tile=tile_irrep,
        pairs=pair_irrep,
    )
    counts = jnp.sum(
        (pair_irrep.reshape(OWNERS, ROWS)[:, :, None] == jnp.arange(8)).astype(I32), axis=1
    )
    rounds = (jnp.max(counts) + SLOTS - 1) // SLOTS
    first = run(jnp.zeros((), I32))
    _, total = lax.while_loop(
        lambda state: state[0] < rounds,
        lambda state: (state[0] + 1, state[1] + run(state[0])),
        (jnp.ones((), I32), first),
    )
    return jnp.transpose(total, (2, 1, 0))


def solution(mesh):
    in_specs = (P("pair", "virt", None), P("virt", "pair", None, None), P(), P(), P())
    out_specs = P("pair", None, "virt")
    return jax.shard_map(body, mesh=mesh, in_specs=in_specs, out_specs=out_specs, check_vma=False)
```
